128 devices in a mesh: prow: 8 (over x, core), pcol: 16 (over y, z).
Axes of the slice: x: 4, y: 4, z: 4, core: 2. Of those that a mesh axis runs over, the one named last changes fastest.
Arguments:
- child_fronts: float32 [8192, 16384], P('prow', 'pcol'), as said below
- parent_own: float32 [16384, 16384], P('prow', 'pcol'), as said below
- pattern: int32 [128, 128], P('prow', 'pcol'), may hold values from 0 to 1, as said below
- child_map: int32 [8, 32], replicated, may hold values from 0 to 127, as said below
Outputs:
- factored_front: float32 [16384, 16384], P('prow', 'pcol')
The draws below stay inside these ranges and needn't reach their ends.
Inputs may be any that keep to these rules, and one draw needn't show every extreme that they name: `child_map`: each row lists 32 distinct parent blocks. In each aligned run of 8 entries of a row, at most 1 lie in any one aligned run of 16 parent blocks, and so at most 1 in any aligned run of 8. `pattern`: Symmetric, with ones on the diagonal. `child_fronts`: each child's tile is symmetric positive definite. `parent_own`: Symmetric; masked by a symmetric pattern with ones on the diagonal it stays positive definite.
All inputs are finite; a program needn't handle non-finite values.
Results may differ from the reference program's by a relative error of at most 0.0001.
Values sent between devices are 32-bit elements; how exact they have to be, the bound alone decides.
No kernel may reach another device: no remote copies, remote signals or barrier semaphores. Data moves between devices by JAX's collectives and lax.ppermute only.
A program may use at most 128 MiB of HBM per device.

```python
import math
import jax
import jax.numpy as jnp
from jax import lax

BLK = 128
PORD = 16384
CORD = 4096
PANB = 4
NPAN = 2
PBLK = 128
CBLK = 32
CDEV = 8
CR = 2
CC = 4
CHILDREN = 8
RSTR = 16


def mirror_tiles(values, upper):
    return jnp.where(upper, values, jnp.transpose(values, (0, 3, 2, 1)))


def coupled_tiles(key, tile_rows, tile_cols, tile_order, weight, coupling):
    subkeys = jax.random.split(key, 5)
    shape_four = (tile_rows, tile_order, tile_cols, tile_order)
    index = jnp.arange(tile_order)
    upper = (index[:, None] < index[None, :])[None, :, None, :]
    on_diag = (index[:, None] == index[None, :])[None, :, None, :]
    distance = jnp.abs(index[:, None] - index[None, :]).astype(jnp.float32)[None, :, None, :]
    reach = 2.0 / (1.0 - math.exp(-2.0))
    spread = 0.8 * reach / (2.0 * math.sqrt(tile_order / 3.0))
    strength = mirror_tiles(jax.random.uniform(subkeys[0], shape_four, jnp.float32, 0.2, 0.5), upper)
    rough = mirror_tiles(jax.random.uniform(subkeys[1], shape_four, jnp.float32, -1.0, 1.0), upper)
    nearby = -strength * jnp.exp(-2.0 * jnp.maximum(distance - 1.0, 0.0))
    extra = jax.random.uniform(subkeys[2], (tile_rows, tile_order, tile_cols), jnp.float32, 0.0, 1.0)
    diagonal = reach * (1.55 + 0.3 * extra)
    filled_tiles = jnp.where(on_diag, diagonal[:, :, :, None], nearby + spread * rough)
    if coupling > 0.0:
        lift = jax.random.uniform(subkeys[4], (tile_rows, tile_order, tile_cols), jnp.float32, 0.5, 1.0)
        outer_lift = lift[:, :, :, None] * jnp.transpose(lift, (0, 2, 1))[:, None, :, :]
        filled_tiles = filled_tiles + coupling * outer_lift
    return (weight * filled_tiles).reshape(tile_rows * tile_order, tile_cols * tile_order)


def draw_child_fronts(key, part):
    return coupled_tiles(key, CR, CC, CORD, 0.5, 0.08)


def draw_parent_own(key, part):
    return coupled_tiles(key, 1, 1, PORD, 1.0, 0.0)


def draw_pattern(key, part):
    drawn_ints = jax.random.randint(key, (PBLK, PBLK), 0, 10)
    pattern_bits = (drawn_ints < 3).astype(jnp.int32)
    pattern_bits = jnp.maximum(pattern_bits, pattern_bits.T)
    on_diag = jnp.arange(PBLK)[:, None] == jnp.arange(PBLK)[None, :]
    return jnp.where(on_diag, 1, pattern_bits).astype(jnp.int32)


def draw_child_map(key, part):
    stripes = PBLK // RSTR
    repeats = max(1, CDEV // stripes)
    subkeys = jax.random.split(key, 2)
    offsets = jax.random.randint(subkeys[0], (CHILDREN, 4), 0, stripes)
    scores = jax.random.randint(subkeys[1], (CHILDREN, stripes, RSTR), 0, 1 << 20) * RSTR + jnp.arange(RSTR)
    orders = jnp.argsort(scores, axis=-1).astype(jnp.int32)
    within = jnp.arange(CDEV)
    stripe_of = (within[None, None, :] + offsets[:, :, None]) % stripes
    repeat_at = jnp.arange(4)[None, :, None] * repeats + within[None, None, :] // stripes
    member = orders[jnp.arange(CHILDREN)[:, None, None], stripe_of, repeat_at]
    return (stripe_of * RSTR + member).reshape(CHILDREN, CBLK).astype(jnp.int32)


def setup_inputs(seed: int = 0) -> dict:
    streams_of = jax.random.split(jax.random.key(seed), 5)
    child_fronts = draw_child_fronts(jax.random.fold_in(streams_of[4], 71), 0)
    parent_own = draw_parent_own(jax.random.fold_in(streams_of[4], 71), 0)
    pattern = draw_pattern(jax.random.fold_in(streams_of[4], 71), 0)
    child_map = draw_child_map(jax.random.fold_in(streams_of[4], 71), 0)
    return dict(child_fronts=child_fronts, parent_own=parent_own, pattern=pattern, child_map=child_map)


def assemble(child_fronts, parent_own, pattern, child_map):
    front_four = parent_own.reshape(PBLK, BLK, PBLK, BLK) * pattern.astype(jnp.float32)[:, None, :, None]
    for child_id in range(CHILDREN):
        row_group = child_id // CC
        col_group = child_id % CC
        child_piece = lax.slice(child_fronts, (row_group * CORD, col_group * CORD), ((row_group + 1) * CORD, (col_group + 1) * CORD))
        child_piece = child_piece.reshape(CBLK, BLK, CBLK, BLK).transpose(0, 2, 1, 3)
        places = child_map[child_id]
        front_four = front_four.at[places[:, None], :, places[None, :], :].add(child_piece)
    return front_four.reshape(PORD, PORD)

def reference(child_fronts, parent_own, pattern, child_map):
    front_tile = assemble(child_fronts, parent_own, pattern, child_map)
    panel_width = PANB * BLK
    for panel_step in range(NPAN):
        start_at = panel_step * panel_width
        end_at = start_at + panel_width
        factor = jnp.linalg.cholesky(front_tile[start_at:end_at, start_at:end_at])
        below_rows = lax.linalg.triangular_solve(factor, front_tile[end_at:, start_at:end_at], left_side=False, lower=True, transpose_a=True)
        trailing = front_tile[end_at:, end_at:] - jnp.dot(below_rows.astype(jnp.float32), below_rows.T.astype(jnp.float32), precision=lax.Precision.HIGHEST, preferred_element_type=jnp.float32)
        front_tile = front_tile.at[end_at:, end_at:].set(trailing)
        front_tile = front_tile.at[start_at:end_at, start_at:end_at].set(factor)
        front_tile = front_tile.at[end_at:, start_at:end_at].set(below_rows)
        front_tile = front_tile.at[start_at:end_at, end_at:].set(0.0)
    return front_tile
```

```python
import jax
import jax.numpy as jnp
from jax import lax
from jax.experimental import pallas as pl
from jax.experimental.pallas import tpu as pltpu
from jax.sharding import PartitionSpec as P

B = 128
NB = 8
W = B * NB
ROWS = 8
COLS = 16
AXES = ("prow", "pcol")
F32 = jnp.float32
BF16 = jnp.bfloat16
HBM = pl.BlockSpec(memory_space=pl.ANY)
SMEM = pl.BlockSpec(memory_space=pltpu.SMEM)
VMEM = pl.BlockSpec(memory_space=pltpu.VMEM)
MIB = 1024 * 1024


def params(mib):
    return pltpu.CompilerParams(vmem_limit_bytes=mib * MIB)


def block(at):
    return pl.ds(pl.multiple_of(at * B, B), B)


def find(cmap, child, group, test):
    at = jnp.int32(-1)
    entry = jnp.int32(0)
    for k in range(8):
        value = cmap[child, group * 8 + k]
        hit = test(value)
        at = jnp.where(hit, k, at)
        entry = jnp.where(hit, value, entry)
    return at, entry


def pack_kernel(ids, cmap, child, bulk, small, sems, small_sems):
    r, c = ids[0], ids[1]
    mine = r // 4 * 4 + c // 4
    gi, gj = r % 4, c % 4
    ja, _ = find(cmap, mine, gj, lambda v: v < 8)
    ia, iv = find(cmap, mine, gi, lambda v: v < 8)
    ja = jnp.maximum(ja, 0)
    ia = jnp.maximum(ia, 0)

    def small_copy(a, slot, k, n):
        return pltpu.make_async_copy(
            child.at[block(a), block(ja)], small.at[slot, k], small_sems.at[n]
        )

    def bulk_copy(n):
        a, b = n // 8, n % 8
        slot = cmap[mine, gi * 8 + a] // 16 * COLS + cmap[mine, gj * 8 + b] // 8
        return pltpu.make_async_copy(child.at[block(a), block(b)], bulk.at[slot], sems.at[n])

    for a in range(8):
        small_copy(a, cmap[mine, gi * 8 + a] // 16, 0, a).start()
    small_copy(ia, jnp.minimum(iv, 7), 1, 8).start()
    lax.fori_loop(0, 64, lambda n, _: (bulk_copy(n).start(), 0)[1], 0)
    for a in range(8):
        small_copy(a, cmap[mine, gi * 8 + a] // 16, 0, a).wait()
    small_copy(ia, jnp.minimum(iv, 7), 1, 8).wait()
    lax.fori_loop(0, 64, lambda n, _: (bulk_copy(n).wait(), 0)[1], 0)


def pack(ids, cmap, child):
    return pl.pallas_call(
        pack_kernel,
        out_shape=(
            jax.ShapeDtypeStruct((ROWS * COLS, B, B), F32),
            jax.ShapeDtypeStruct((ROWS, 2, B, B), F32),
        ),
        in_specs=[SMEM, SMEM, HBM],
        out_specs=(HBM, HBM),
        scratch_shapes=[pltpu.SemaphoreType.DMA((64,)), pltpu.SemaphoreType.DMA((9,))],
        name="pack",
    )(ids, cmap, child)


def relay_kernel(ids, cmap, came, owners, diag, sems):
    r, c = ids[0], ids[1]
    copies = []
    for half in range(2):
        child = half * 4 + c // 4
        pick = jnp.int32(half * 4)
        for k in range(4):
            src = half * 4 + k
            _, entry = find(cmap, child, k, lambda v: v // 16 == r)
            copies.append((came.at[src, 0], owners.at[entry % 16, half]))
            at, _ = find(cmap, child, k, lambda v: v == r)
            pick = jnp.where(at >= 0, src, pick)
        copies.append((came.at[pick, 1], diag.at[half]))
    made = [pltpu.make_async_copy(s, d, sems.at[n]) for n, (s, d) in enumerate(copies)]
    for m in made:
        m.start()
    for m in made:
        m.wait()


def relay(ids, cmap, came):
    return pl.pallas_call(
        relay_kernel,
        out_shape=(
            jax.ShapeDtypeStruct((COLS, 2, B, B), F32),
            jax.ShapeDtypeStruct((2, B, B), F32),
        ),
        in_specs=[SMEM, SMEM, HBM],
        out_specs=(HBM, HBM),
        scratch_shapes=[pltpu.SemaphoreType.DMA((10,))],
        name="relay",
    )(ids, cmap, came)


def gather_rows(cmap, wanted, start, came, out):
    for k in range(NB):
        out[:, k * B : (k + 1) * B] = start[k * B : (k + 1) * B, :].T
    for child in range(8):
        half, quarter = child // 4, child % 4
        hit = lax.fori_loop(
            0, 32, lambda n, h: h | (cmap[child, n] == wanted).astype(jnp.int32), jnp.int32(0)
        )

        @pl.when(hit > 0)
        def _():
            for g in range(4):
                at, entry = find(cmap, child, g, lambda v: v < 8)

                @pl.when(at >= 0)
                def _():
                    where = block(jnp.minimum(entry, 7))
                    out[:, where] = out[:, where] + came[quarter * 4 + g, half]


def owner_kernel(ids, cmap, start, came, out):
    gather_rows(cmap, ids[0] * COLS + ids[1], start, came, out)


def diag_kernel(ids, cmap, start, came, out):
    gather_rows(cmap, ids[0], start, came, out)


def assemble(kernel, name, ids, cmap, start, came):
    return pl.pallas_call(
        kernel,
        out_shape=jax.ShapeDtypeStruct((B, W), F32),
        in_specs=[SMEM, SMEM, VMEM, VMEM],
        out_specs=VMEM,
        compiler_params=params(24),
        name=name,
    )(ids, cmap, start, came)


def spread_lane(x, k):
    return jnp.broadcast_to(x[:, k : k + 1], (8, B))


def spread_sub(x, k):
    return jnp.broadcast_to(x[k : k + 1, :], (8, B))


def eliminate_block(strips):
    sub = lax.broadcasted_iota(jnp.int32, (8, B), 0)
    lane = lax.broadcasted_iota(jnp.int32, (8, B), 1)
    strips = list(strips)
    for m in range(16):
        first = 8 * m
        inside = (lane >= first) & (lane < first + 8)
        w = strips[m]
        cols = [spread_lane(w, first + k) for k in range(8)]
        scales, rows, mults = [], [], []
        for k in range(8):
            rs = lax.rsqrt(spread_sub(cols[k], k))
            row = jnp.where(lane == first + k, rs, spread_sub(w, k) * rs)
            p = cols[k] * rs
            mult = [spread_sub(p, q) for q in range(k + 1, 8)]
            for n, q in enumerate(range(k + 1, 8)):
                cols[q] = cols[q] - p * mult[n]
            rest = jnp.where(lane == first + k, 0.0, w) - p * row
            w = jnp.where(sub > k, rest, jnp.where(sub == k, row, w))
            scales.append(rs)
            rows.append(jnp.where(inside & (lane > first + k), 0.0, row))
            mults.append(mult)
        strips[m] = w
        for s in range(m + 1, 16):
            v = strips[s]
            below = [spread_lane(v, first + k) for k in range(8)]
            v = jnp.where(inside, 0.0, v)
            for k in range(8):
                p = below[k] * scales[k]
                v = v - p * rows[k]
                for n, q in enumerate(range(k + 1, 8)):
                    below[q] = below[q] - p * mults[k][n]
            strips[s] = v
    return strips


def dot32(a, b, ca, cb):
    return lax.dot_general(
        a, b, (((ca,), (cb,)), ((), ())), precision=lax.Precision.HIGHEST, preferred_element_type=F32
    )


def factor_kernel(a_ref, w_ref, d_ref, q_ref):
    row = lax.broadcasted_iota(jnp.int32, (B, B), 0)
    col = lax.broadcasted_iota(jnp.int32, (B, B), 1)
    w_ref[...] = a_ref[...]

    def step(kb, _):
        here = block(kb)
        d_ref[...] = w_ref[here, here]
        strips = eliminate_block([d_ref[8 * s : 8 * s + 8, :] for s in range(16)])
        for s in range(16):
            d_ref[8 * s : 8 * s + 8, :] = strips[s]
        inverse = jnp.where(row >= col, d_ref[...], 0.0)
        q_ref[...] = dot32(inverse, w_ref[here, :], 1, 0)
        q_ref[:, here] = inverse

        def below(i, _):
            rows = block(i)
            w_ref[rows, here] = jnp.zeros((B, B), F32)
            w_ref[rows, :] = w_ref[rows, :] - dot32(q_ref[:, rows], q_ref[...], 0, 0)
            return 0

        lax.fori_loop(kb + 1, NB, below, 0)
        w_ref[here, :] = q_ref[...]
        w_ref[here, here] = d_ref[...]
        return 0

    lax.fori_loop(0, NB, step, 0)


def factor(a):
    return pl.pallas_call(
        factor_kernel,
        out_shape=jax.ShapeDtypeStruct((W, W), F32),
        in_specs=[VMEM],
        out_specs=VMEM,
        scratch_shapes=[pltpu.VMEM((B, B), F32), pltpu.VMEM((B, W), F32)],
        compiler_params=params(32),
        name="factor",
    )(a)


def halves(x):
    high = x.astype(BF16)
    return high, (x - high.astype(F32)).astype(BF16)


def dot_nt(a, b):
    return lax.dot_general(a, b, (((1,), (1,)), ((), ())), preferred_element_type=F32)


def dot3(ah, al, bh, bl):
    return dot_nt(ah, bh) + (dot_nt(ah, bl) + dot_nt(al, bh))


SOLVE = 256
CHUNK = 256


def solve_rows(raw, out, eh, el):
    xh, xl = halves(raw)
    for j in range(W // SOLVE):
        upto = (j + 1) * SOLVE
        rows = slice(j * SOLVE, upto)
        out[:, rows] = dot3(xh[:, :upto], xl[:, :upto], eh[rows, :upto], el[rows, :upto])


def update_kernel(ids, pattern, w_ref, xc_ref, xr_ref, own_ref, out_ref, eh, el, ch, cl, x):
    step = pl.program_id(0)
    r, c = ids[0], ids[1]

    @pl.when(step == 0)
    def _():
        row = lax.broadcasted_iota(jnp.int32, (B, W), 0)
        col = lax.broadcasted_iota(jnp.int32, (B, W), 1)

        def split(i, _):
            rows = block(i)
            high, low = halves(jnp.where(row + i * B >= col, w_ref[rows, :], 0.0))
            eh[rows, :] = high
            el[rows, :] = low
            return 0

        lax.fori_loop(0, NB, split, 0)

        def columns(i, _):
            rows = pl.ds(pl.multiple_of(i * CHUNK, CHUNK), CHUNK)
            solve_rows(xc_ref[rows, :], x, eh, el)
            high, low = halves(x[...])
            ch[rows, :] = high
            cl[rows, :] = low
            return 0

        lax.fori_loop(0, W // CHUNK, columns, 0)

    solve_rows(xr_ref[...], x, eh, el)
    top = (r == 0) & (step < W // CHUNK)

    @pl.when((c > 0) & top)
    def _():
        out_ref[...] = jnp.zeros_like(out_ref)

    @pl.when((c > 0) & jnp.logical_not(top))
    def _():
        high, low = halves(x[...])
        for j in range(W // SOLVE):
            cols = slice(j * SOLVE, (j + 1) * SOLVE)
            change = dot3(high, low, ch[cols, :], cl[cols, :])
            for a in range(CHUNK // B):
                for b in range(SOLVE // B):
                    rs = slice(a * B, (a + 1) * B)
                    at = j * (SOLVE // B) + b
                    cs = slice(at * B, (at + 1) * B)
                    keep = pattern[step * (CHUNK // B) + a, at].astype(F32)
                    out_ref[rs, cs] = own_ref[rs, cs] * keep - change[rs, b * B : (b + 1) * B]

    @pl.when((c == 0) & jnp.logical_not(top))
    def _():
        out_ref[...] = x[...]

    @pl.when((c == 0) & top)
    def _():
        row = lax.broadcasted_iota(jnp.int32, (CHUNK, B), 0)
        col = lax.broadcasted_iota(jnp.int32, (CHUNK, B), 1)
        for j in range(NB):
            cols = slice(j * B, (j + 1) * B)
            rows = pl.ds(pl.multiple_of(step * CHUNK, CHUNK), CHUNK)
            above = w_ref[cols, rows].T
            here = w_ref[rows, cols]
            gap = row + step * CHUNK - (col + j * B)
            out_ref[:, cols] = jnp.where(gap > 0, above, jnp.where(gap == 0, 1.0 / here, 0.0))


def update(ids, pattern, w, xc, xr, own):
    rows = own.shape[0]
    whole = pl.BlockSpec((W, W), lambda i: (0, 0), pipeline_mode=pl.Buffered(1))
    part = pl.BlockSpec((CHUNK, W), lambda i: (i, 0))
    return pl.pallas_call(
        update_kernel,
        grid=(rows // CHUNK,),
        out_shape=jax.ShapeDtypeStruct(own.shape, F32),
        in_specs=[SMEM, SMEM, whole, whole, part, part],
        out_specs=part,
        scratch_shapes=[pltpu.VMEM((W, W), BF16)] * 4 + [pltpu.VMEM((CHUNK, W), F32)],
        compiler_params=params(48),
        name="update",
    )(ids, pattern, w, xc, xr, own)


def add_kernel(ids, cmap, came, base, out, tile, parts, tile_sem, sems):
    r, c = ids[0], ids[1]
    load = pltpu.make_async_copy(base, tile, tile_sem)
    load.start()

    def visit(n, act):
        src_r, src_c = n // COLS, n % COLS
        child = src_r // 4 * 4 + src_c // 4
        ra, rv = find(cmap, child, src_r % 4, lambda v: v // 16 == r)
        ca, cv = find(cmap, child, src_c % 4, lambda v: v // 8 == c)
        low, col = rv % 16, cv % 8
        ok = (ra >= 0) & (ca >= 0) & (c > 0) & ((r > 0) | (low >= 8))

        @pl.when(ok)
        def _():
            act(n, low, col)

        return 0

    def copy(n):
        return pltpu.make_async_copy(came.at[n], parts.at[n], sems.at[n])

    def begin(n, low, col):
        copy(n).start()

    def finish(n, low, col):
        copy(n).wait()
        rows, cols = block(low), block(col)
        tile[rows, cols] = tile[rows, cols] + parts[n]

    lax.fori_loop(0, ROWS * COLS, lambda n, _: visit(n, begin), 0)
    load.wait()
    lax.fori_loop(0, ROWS * COLS, lambda n, _: visit(n, finish), 0)
    store = pltpu.make_async_copy(tile, out, tile_sem)
    store.start()
    store.wait()


def add(ids, cmap, came, base):
    return pl.pallas_call(
        add_kernel,
        out_shape=jax.ShapeDtypeStruct(base.shape, F32),
        in_specs=[SMEM, SMEM, HBM, HBM],
        out_specs=HBM,
        scratch_shapes=[
            pltpu.VMEM(base.shape, F32),
            pltpu.VMEM((ROWS * COLS, B, B), F32),
            pltpu.SemaphoreType.DMA(()),
            pltpu.SemaphoreType.DMA((ROWS * COLS,)),
        ],
        compiler_params=params(32),
        name="add",
    )(ids, cmap, came, base)


def at(r, c):
    return r * COLS + c


def body(child, own, pattern, cmap):
    ids = jnp.stack([lax.axis_index("prow"), lax.axis_index("pcol")]).astype(jnp.int32)
    bulk, small = pack(ids, cmap, child)
    small = lax.all_to_all(small, "prow", 0, 0, tiled=True)

    start = None
    keep = jnp.repeat(pattern[:NB].astype(F32), B, axis=0)
    for k in range(NB):
        piece = own[:W, k * B : (k + 1) * B] * keep[:, k : k + 1]
        moves = [(at(0, c), at(c // 2, 8 * (c % 2) + k)) for c in range(COLS)]
        piece = lax.ppermute(piece, AXES, moves)
        mine = lax.axis_index("pcol") % 8 == k
        start = jnp.where(mine, piece, 0.0 if start is None else start)
    diag_start = lax.ppermute(start, AXES, [(at(0, k), at(k, 0)) for k in range(NB)])
    diag_start = lax.all_to_all(diag_start, "pcol", 0, 0, tiled=True)[: W // COLS]
    diag_start = lax.all_gather(diag_start, "pcol", axis=0, tiled=True)

    owners, diag = relay(ids, cmap, small)
    diag = lax.all_gather(diag, "pcol", axis=0).reshape(COLS, 2, B, B)
    owners = lax.all_to_all(owners, "pcol", 0, 0, tiled=True)

    diag_rows = assemble(diag_kernel, "diag_rows", ids, cmap, diag_start, diag)
    pivot = lax.all_gather(diag_rows, "prow", axis=0, tiled=True)
    owned = assemble(owner_kernel, "owner_rows", ids, cmap, start, owners)
    moves = [
        (at(r, c), at(c % 8, 2 * r + c // 8)) for r in range(ROWS) for c in range(COLS)
    ]
    xc = lax.ppermute(owned, AXES, moves)
    xc = lax.all_gather(xc, "prow", axis=0, tiled=True)
    xr = lax.all_gather(owned, "pcol", axis=0, tiled=True)

    bulk = lax.all_to_all(bulk, AXES, 0, 0, tiled=True)
    w = factor(pivot)
    base = update(ids, pattern, w, xc, xr, own)
    return add(ids, cmap, bulk, base)


def solution(mesh):
    return jax.shard_map(
        body,
        mesh=mesh,
        in_specs=(P("prow", "pcol"), P("prow", "pcol"), P("prow", "pcol"), P()),
        out_specs=P("prow", "pcol"),
        check_vma=False,
    )
```

```python
import jax
import jax.numpy as jnp
from jax import lax
from jax.experimental import pallas as pl
from jax.experimental.pallas import tpu as pltpu
from jax.sharding import PartitionSpec as P

B = 128
NB = 8
W = B * NB
ROWS = 8
COLS = 16
AXES = ("prow", "pcol")
F32 = jnp.float32
BF16 = jnp.bfloat16
HBM = pl.BlockSpec(memory_space=pltpu.HBM)
SMEM = pl.BlockSpec(memory_space=pltpu.SMEM)
VMEM = pl.BlockSpec(memory_space=pltpu.VMEM)
MIB = 1024 * 1024
PARTS = 4
PART = B // PARTS


def params(mib):
    return pltpu.CompilerParams(vmem_limit_bytes=mib * MIB)


def block(at):
    return pl.ds(pl.multiple_of(at * B, B), B)


def find(cmap, child, group, test):
    at = jnp.int32(-1)
    entry = jnp.int32(0)
    for k in range(8):
        value = cmap[child, group * 8 + k]
        hit = test(value)
        at = jnp.where(hit, k, at)
        entry = jnp.where(hit, value, entry)
    return at, entry


def pack_small_kernel(ids, cmap, child, *rest):
    outs, sems = rest[:ROWS], rest[ROWS]
    r, c = ids[0], ids[1]
    mine = r // 4 * 4 + c // 4
    ja, _ = find(cmap, mine, c % 4, lambda v: v < 8)
    ia, _ = find(cmap, mine, r % 4, lambda v: v < 8)
    ja = jnp.maximum(ja, 0)
    ia = jnp.maximum(ia, 0)
    made = []
    for d in range(ROWS):
        a, _ = find(cmap, mine, r % 4, lambda v: v // 16 == (r + d) % ROWS)
        for k, row in enumerate((jnp.maximum(a, 0), ia)):
            src = child.at[block(row), block(ja)]
            made.append(pltpu.make_async_copy(src, outs[d].at[k], sems.at[2 * d + k]))
    for m in made:
        m.start()
    for m in made:
        m.wait()


def pack_small(ids, cmap, child):
    return pl.pallas_call(
        pack_small_kernel,
        out_shape=(jax.ShapeDtypeStruct((2, B, B), F32),) * ROWS,
        in_specs=[SMEM, SMEM, VMEM],
        out_specs=(HBM,) * ROWS,
        scratch_shapes=[pltpu.SemaphoreType.DMA((2 * ROWS,))],
        compiler_params=params(12),
        name="pack_small",
    )(ids, cmap, child)


def pack_kernel(ids, cmap, child, *rest):
    bulk, sems = rest[:PARTS], rest[PARTS]
    r, c = ids[0], ids[1]
    mine = r // 4 * 4 + c // 4
    gi, gj = r % 4, c % 4

    def copies(n):
        a, b = n // 8, n % 8
        slot = cmap[mine, gi * 8 + a] // 16 * COLS + cmap[mine, gj * 8 + b] // 8
        for part in range(PARTS):
            rows = pl.ds(pl.multiple_of(a * B + part * PART, PART), PART)
            src = child.at[rows, block(b)]
            yield pltpu.make_async_copy(src, bulk[part].at[slot], sems.at[n, part])

    def start(n, _):
        for m in copies(n):
            m.start()
        return 0

    def wait(n, _):
        for m in copies(n):
            m.wait()
        return 0

    lax.fori_loop(0, 64, start, 0)
    lax.fori_loop(0, 64, wait, 0)


def pack(ids, cmap, child):
    return pl.pallas_call(
        pack_kernel,
        out_shape=(jax.ShapeDtypeStruct((ROWS * COLS, PART, B), F32),) * PARTS,
        in_specs=[SMEM, SMEM, VMEM],
        out_specs=(HBM,) * PARTS,
        scratch_shapes=[pltpu.SemaphoreType.DMA((64, PARTS))],
        compiler_params=params(60),
        name="pack",
    )(ids, cmap, child)


def relay_kernel(ids, cmap, *rest):
    came, outs, sems = rest[:ROWS], rest[ROWS : ROWS + COLS], rest[ROWS + COLS]
    r, c = ids[0], ids[1]
    source, goes = [], []
    for d in range(ROWS):
        src = (r + ROWS - d) % ROWS
        child = src // 4 * 4 + c // 4
        _, entry = find(cmap, child, src % 4, lambda v: v // 16 == r)
        source.append(src // 4)
        goes.append((entry % 16 - c + COLS) % COLS)

    def each(act):
        for d in range(ROWS):
            for e in range(COLS):

                @pl.when(goes[d] == e)
                def _():
                    act(pltpu.make_async_copy(came[d].at[0], outs[e].at[source[d]], sems.at[d]))

    each(lambda m: m.start())
    each(lambda m: m.wait())


def relay(ids, cmap, came):
    return pl.pallas_call(
        relay_kernel,
        out_shape=(jax.ShapeDtypeStruct((2, B, B), F32),) * COLS,
        in_specs=[SMEM, SMEM] + [VMEM] * ROWS,
        out_specs=(HBM,) * COLS,
        scratch_shapes=[pltpu.SemaphoreType.DMA((ROWS,))],
        compiler_params=params(12),
        name="relay",
    )(ids, cmap, *came)


def relay_diag_kernel(ids, cmap, *rest):
    came, out = rest[:ROWS], rest[ROWS]
    r, c = ids[0], ids[1]
    for d in range(ROWS):
        src = (r + ROWS - d) % ROWS
        child = src // 4 * 4 + c // 4
        at, _ = find(cmap, child, src % 4, lambda v: v == r)

        @pl.when(at >= 0)
        def _():
            out[src // 4] = came[d][1]


def relay_diag(ids, cmap, came):
    return pl.pallas_call(
        relay_diag_kernel,
        out_shape=jax.ShapeDtypeStruct((2, B, B), F32),
        in_specs=[SMEM, SMEM] + [VMEM] * ROWS,
        out_specs=VMEM,
        compiler_params=params(12),
        name="relay_diag",
    )(ids, cmap, *came)


def listed(cmap, child, wanted):
    hit = lax.fori_loop(
        0, 32, lambda n, h: h | (cmap[child, n] == wanted).astype(jnp.int32), jnp.int32(0)
    )
    return hit > 0


def add_block(cmap, child, group, ok, part, out):
    at, entry = find(cmap, child, group, lambda v: v < 8)

    @pl.when(ok & (at >= 0))
    def _():
        where = block(jnp.minimum(entry, 7))
        out[:, where] = out[:, where] + part[...]


def owner_kernel(ids, cmap, start, *rest):
    came, out = rest[:COLS], rest[COLS]
    r, c = ids[0], ids[1]
    for k in range(NB):
        out[:, k * B : (k + 1) * B] = start[k * B : (k + 1) * B, :].T
    ok = [listed(cmap, child, r * COLS + c) for child in range(8)]
    for d in range(COLS):
        src = (c + COLS - d) % COLS
        for half in range(2):
            hit = jnp.bool_(False)
            for q in range(4):
                hit = hit | (ok[half * 4 + q] & (src // 4 == q))
            add_block(cmap, half * 4 + src // 4, src % 4, hit, came[d].at[half], out)


def owner_rows(ids, cmap, start, came):
    return pl.pallas_call(
        owner_kernel,
        out_shape=jax.ShapeDtypeStruct((B, W), F32),
        in_specs=[SMEM, SMEM, VMEM] + [VMEM] * COLS,
        out_specs=VMEM,
        compiler_params=params(24),
        name="owner_rows",
    )(ids, cmap, start, *came)


def diag_kernel(ids, cmap, parent, came, out):
    for k in range(NB):
        out[:, k * B : (k + 1) * B] = parent[k]
    for child in range(8):
        ok = listed(cmap, child, ids[0])
        for g in range(4):
            add_block(cmap, child, g, ok, came.at[child % 4 * 4 + g, child // 4], out)


def diag_rows(ids, cmap, parent, came):
    return pl.pallas_call(
        diag_kernel,
        out_shape=jax.ShapeDtypeStruct((B, W), F32),
        in_specs=[SMEM, SMEM, VMEM, VMEM],
        out_specs=VMEM,
        compiler_params=params(24),
        name="diag_rows",
    )(ids, cmap, parent, came)


def spread_lane(x, k):
    return jnp.broadcast_to(x[:, k : k + 1], (8, B))


def spread_sub(x, k):
    return jnp.broadcast_to(x[k : k + 1, :], (8, B))


def eliminate_block(strips):
    sub = lax.broadcasted_iota(jnp.int32, (8, B), 0)
    lane = lax.broadcasted_iota(jnp.int32, (8, B), 1)
    strips = list(strips)
    for m in range(16):
        first = 8 * m
        inside = (lane >= first) & (lane < first + 8)
        w = strips[m]
        cols = [spread_lane(w, first + k) for k in range(8)]
        scales, rows, mults = [], [], []
        for k in range(8):
            rs = lax.rsqrt(spread_sub(cols[k], k))
            row = jnp.where(lane == first + k, rs, spread_sub(w, k) * rs)
            p = cols[k] * rs
            mult = [spread_sub(p, q) for q in range(k + 1, 8)]
            for n, q in enumerate(range(k + 1, 8)):
                cols[q] = cols[q] - p * mult[n]
            rest = jnp.where(lane == first + k, 0.0, w) - p * row
            w = jnp.where(sub > k, rest, jnp.where(sub == k, row, w))
            scales.append(rs)
            rows.append(jnp.where(inside & (lane > first + k), 0.0, row))
            mults.append(mult)
        strips[m] = w
        for s in range(m + 1, 16):
            v = strips[s]
            below = [spread_lane(v, first + k) for k in range(8)]
            v = jnp.where(inside, 0.0, v)
            for k in range(8):
                p = below[k] * scales[k]
                v = v - p * rows[k]
                for n, q in enumerate(range(k + 1, 8)):
                    below[q] = below[q] - p * mults[k][n]
            strips[s] = v
    return strips


def dot32(a, b, ca, cb):
    return lax.dot_general(
        a, b, (((ca,), (cb,)), ((), ())), precision=lax.Precision.HIGHEST, preferred_element_type=F32
    )


def factor_kernel(a_ref, w_ref, d_ref, q_ref):
    row = lax.broadcasted_iota(jnp.int32, (B, B), 0)
    col = lax.broadcasted_iota(jnp.int32, (B, B), 1)
    w_ref[...] = a_ref[...]

    def step(kb, _):
        here = block(kb)
        d_ref[...] = w_ref[here, here]
        strips = eliminate_block([d_ref[8 * s : 8 * s + 8, :] for s in range(16)])
        for s in range(16):
            d_ref[8 * s : 8 * s + 8, :] = strips[s]
        inverse = jnp.where(row >= col, d_ref[...], 0.0)
        q_ref[...] = dot32(inverse, w_ref[here, :], 1, 0)
        q_ref[:, here] = inverse

        def below(i, _):
            rows = block(i)
            w_ref[rows, here] = jnp.zeros((B, B), F32)
            w_ref[rows, :] = w_ref[rows, :] - dot32(q_ref[:, rows], q_ref[...], 0, 0)
            return 0

        lax.fori_loop(kb + 1, NB, below, 0)
        w_ref[here, :] = q_ref[...]
        w_ref[here, here] = d_ref[...]
        return 0

    lax.fori_loop(0, NB, step, 0)


def factor(a):
    return pl.pallas_call(
        factor_kernel,
        out_shape=jax.ShapeDtypeStruct((W, W), F32),
        in_specs=[VMEM],
        out_specs=VMEM,
        scratch_shapes=[pltpu.VMEM((B, B), F32), pltpu.VMEM((B, W), F32)],
        compiler_params=params(32),
        name="factor",
    )(a)


def halves(x):
    high = x.astype(BF16)
    return high, (x - high.astype(F32)).astype(BF16)


def dot_nt(a, b):
    return lax.dot_general(a, b, (((1,), (1,)), ((), ())), preferred_element_type=F32)


def dot3(ah, al, bh, bl):
    return dot_nt(ah, bh) + (dot_nt(ah, bl) + dot_nt(al, bh))


SOLVE = 256
CHUNK = 256


def solve_rows(raw, out, eh, el):
    xh, xl = halves(raw)
    for j in range(W // SOLVE):
        upto = (j + 1) * SOLVE
        rows = slice(j * SOLVE, upto)
        out[:, rows] = dot3(xh[:, :upto], xl[:, :upto], eh[rows, :upto], el[rows, :upto])


def update_kernel(ids, w_ref, xc_ref, xr_ref, own_ref, out_ref, eh, el, ch, cl, x):
    step = pl.program_id(0)
    r, c = ids[0], ids[1]

    @pl.when(step == 0)
    def _():
        row = lax.broadcasted_iota(jnp.int32, (B, W), 0)
        col = lax.broadcasted_iota(jnp.int32, (B, W), 1)

        def split(i, _):
            rows = block(i)
            high, low = halves(jnp.where(row + i * B >= col, w_ref[rows, :], 0.0))
            eh[rows, :] = high
            el[rows, :] = low
            return 0

        lax.fori_loop(0, NB, split, 0)

        def columns(i, _):
            rows = pl.ds(pl.multiple_of(i * CHUNK, CHUNK), CHUNK)
            solve_rows(xc_ref[rows, :], x, eh, el)
            high, low = halves(x[...])
            ch[rows, :] = high
            cl[rows, :] = low
            return 0

        lax.fori_loop(0, W // CHUNK, columns, 0)

    solve_rows(xr_ref[...], x, eh, el)
    top = (r == 0) & (step < W // CHUNK)

    @pl.when((c > 0) & top)
    def _():
        out_ref[...] = jnp.zeros_like(out_ref)

    @pl.when((c > 0) & jnp.logical_not(top))
    def _():
        high, low = halves(x[...])
        for j in range(W // SOLVE):
            cols = slice(j * SOLVE, (j + 1) * SOLVE)
            change = dot3(high, low, ch[cols, :], cl[cols, :])
            out_ref[:, cols] = own_ref[:, cols] - change

    @pl.when((c == 0) & jnp.logical_not(top))
    def _():
        out_ref[...] = x[...]

    @pl.when((c == 0) & top)
    def _():
        row = lax.broadcasted_iota(jnp.int32, (CHUNK, B), 0)
        col = lax.broadcasted_iota(jnp.int32, (CHUNK, B), 1)
        for j in range(NB):
            cols = slice(j * B, (j + 1) * B)
            rows = pl.ds(pl.multiple_of(step * CHUNK, CHUNK), CHUNK)
            above = w_ref[cols, rows].T
            here = w_ref[rows, cols]
            gap = row + step * CHUNK - (col + j * B)
            out_ref[:, cols] = jnp.where(gap > 0, above, jnp.where(gap == 0, 1.0 / here, 0.0))


def update(ids, w, xc, xr, own):
    rows = own.shape[0]
    whole = pl.BlockSpec((W, W), lambda i: (0, 0), pipeline_mode=pl.Buffered(1))
    part = pl.BlockSpec((CHUNK, W), lambda i: (i, 0))
    return pl.pallas_call(
        update_kernel,
        grid=(rows // CHUNK,),
        out_shape=jax.ShapeDtypeStruct(own.shape, F32),
        in_specs=[SMEM, whole, whole, part, part],
        out_specs=part,
        scratch_shapes=[pltpu.VMEM((W, W), BF16)] * 4 + [pltpu.VMEM((CHUNK, W), F32)],
        compiler_params=params(60),
        name="update",
    )(ids, w, xc, xr, own)


def add_kernel(ids, pattern, cmap, *rest):
    came, (own, out, tile, held, places, tile_sem, sems) = rest[:PARTS], rest[PARTS:]
    r, c = ids[0], ids[1]
    load = pltpu.make_async_copy(own, tile, tile_sem)
    load.start()

    def table(n, _):
        ra, rv = find(cmap, n // 4, n % 4, lambda v: v // 16 == r)
        ca, cv = find(cmap, n // 4, n % 4, lambda v: v // 8 == c)
        low = rv % 16
        rok = (ra >= 0) & ((r > 0) | (low >= 8))
        cok = (ca >= 0) & (c > 0)
        places[0, n] = jnp.where(rok, low, -1)
        places[1, n] = jnp.where(cok, cv % 8, -1)
        return 0

    lax.fori_loop(0, 32, table, 0)

    def copies(n):
        for part in range(PARTS):
            dst = held.at[n, pl.ds(part * PART, PART)]
            yield pltpu.make_async_copy(came[part].at[n], dst, sems.at[n, part])

    def visit(act):
        def one(n, _):
            src_r, src_c = n // COLS, n % COLS
            child = src_r // 4 * 4 + src_c // 4
            low = places[0, child * 4 + src_r % 4]
            col = places[1, child * 4 + src_c % 4]

            @pl.when((low >= 0) & (col >= 0))
            def _():
                act(n, low, col)

            return 0

        lax.fori_loop(0, ROWS * COLS, one, 0)

    def begin(n, low, col):
        for m in copies(n):
            m.start()

    def finish(n, low, col):
        for m in copies(n):
            m.wait()
        rows, cols = block(low), block(col)
        tile[rows, cols] = tile[rows, cols] + held[n]

    visit(begin)
    load.wait()

    def mask(n, _):
        i, j = n // 8, n % 8

        @pl.when(pattern[i, j] == 0)
        def _():
            tile[block(i), block(j)] = jnp.zeros((B, B), F32)

        return 0

    lax.fori_loop(0, 128, mask, 0)
    visit(finish)
    store = pltpu.make_async_copy(tile, out, tile_sem)
    store.start()
    store.wait()


def add(ids, pattern, cmap, came, own):
    return pl.pallas_call(
        add_kernel,
        out_shape=jax.ShapeDtypeStruct(own.shape, F32),
        in_specs=[SMEM, SMEM, SMEM] + [HBM] * (PARTS + 1),
        out_specs=HBM,
        scratch_shapes=[
            pltpu.VMEM(own.shape, F32),
            pltpu.VMEM((ROWS * COLS, B, B), F32),
            pltpu.SMEM((2, 32), jnp.int32),
            pltpu.SemaphoreType.DMA(()),
            pltpu.SemaphoreType.DMA((ROWS * COLS, PARTS)),
        ],
        compiler_params=params(60),
        name="add",
    )(ids, pattern, cmap, *came, own)


def at(r, c):
    return r * COLS + c


def shift(parts, axis, count):
    return [parts[0]] + [
        lax.ppermute(parts[d], axis, [(k, (k + d) % count) for k in range(count)])
        for d in range(1, count)
    ]


def after(value, first):
    return lax.optimization_barrier((value, first))[0]


def body(child, own, pattern, cmap):
    ids = jnp.stack([lax.axis_index("prow"), lax.axis_index("pcol")]).astype(jnp.int32)

    row, col = ids[0], ids[1]
    small = pack_small(ids, cmap, child)
    bulk = pack(ids, cmap, child)
    came = shift(small, "prow", ROWS)

    keep = pattern[:NB].astype(F32)
    start = None
    turn = (col % NB - (2 * row + col // NB) // 2) % NB
    for k in range(NB):
        n = (k + col // 2) % NB
        mask = jnp.repeat(lax.dynamic_slice_in_dim(keep, n, 1, 1), B, axis=0)
        piece = lax.dynamic_slice_in_dim(own, n * B, B, 1)[:W] * mask
        moves = [(at(0, c), at(c // 2, 8 * (c % 2) + (k + c // 2) % NB)) for c in range(COLS)]
        piece = lax.ppermute(piece, AXES, moves)
        start = jnp.where(turn == k, piece, 0.0 if start is None else start)
    top = jnp.where(row == 0, start, 0.0).reshape(NB, B, B)
    parent = lax.psum_scatter(top, "prow", scatter_dimension=0, tiled=True)
    parent = lax.all_gather(parent, "pcol", axis=0, tiled=True)

    done = []

    def part(first, values):
        sent = after(bulk[len(done)], first)
        got = lax.all_to_all(sent, AXES, 0, 0, tiled=True)
        values, got = lax.optimization_barrier((values, got))
        done.append(got)
        return values

    diag = relay_diag(ids, cmap, came)
    diag_all = lax.all_gather(diag, "pcol", axis=0)
    owners = shift(relay(ids, cmap, part(diag, came)), "pcol", COLS)
    pivot = diag_rows(ids, cmap, parent, after(diag_all, owners))
    pivot = lax.all_gather(pivot, "prow", axis=0, tiled=True)
    owned = owner_rows(ids, cmap, start, part(done[0], owners))
    moves = [
        (at(r, c), at(c % 8, 2 * r + c // 8)) for r in range(ROWS) for c in range(COLS)
    ]
    xc = lax.ppermute(owned, AXES, moves)
    xc = lax.all_gather(xc, "prow", axis=0, tiled=True)
    xr = lax.all_gather(owned, "pcol", axis=0, tiled=True)

    w = factor(part(owned, pivot))
    w = part(done[2], w)
    base = add(ids, pattern, cmap, done, own)
    return update(ids, w, xc, xr, base)


def solution(mesh):
    return jax.shard_map(
        body,
        mesh=mesh,
        in_specs=(P("prow", "pcol"), P("prow", "pcol"), P("prow", "pcol"), P()),
        out_specs=P("prow", "pcol"),
        check_vma=False,
    )
```

```python
import jax
import jax.numpy as jnp
import numpy as np
from jax import lax
from jax.experimental import pallas as pl
from jax.experimental.pallas import tpu as pltpu
from jax.sharding import PartitionSpec as P

B = 128
NB = 8
W = B * NB
ROWS = 8
COLS = 16
AXES = ("prow", "pcol")
F32 = jnp.float32
BF16 = jnp.bfloat16
HBM = pl.BlockSpec(memory_space=pltpu.HBM)
SMEM = pl.BlockSpec(memory_space=pltpu.SMEM)
VMEM = pl.BlockSpec(memory_space=pltpu.VMEM)
MIB = 1024 * 1024


def params(mib):
    return pltpu.CompilerParams(vmem_limit_bytes=mib * MIB)


def block(at):
    return pl.ds(pl.multiple_of(at * B, B), B)


def find(cmap, child, group, test):
    at = jnp.int32(-1)
    entry = jnp.int32(0)
    for k in range(8):
        value = cmap[child, group * 8 + k]
        hit = test(value)
        at = jnp.where(hit, k, at)
        entry = jnp.where(hit, value, entry)
    return at, entry


def scatter_plan():
    queues = {}
    for r in range(ROWS):
        for c in range(1, COLS):
            if r == 0 and c < 8:
                move = ((0, 0), 0, c)
            elif c % 8 < 5:
                move = ((0, 2 * r + c // 8), 0, c % 8)
            else:
                move = ((r, 0), 1, c)
            queues.setdefault(move[0], []).append((move[1], move[2], (r, c)))
    steps = max(len(q) for q in queues.values())
    moves = [[] for _ in range(steps)]
    sends = np.zeros((ROWS * COLS, steps, 2), np.int32)
    gets = np.zeros((ROWS * COLS, 2), np.int32)
    gets[:, 0] = -1
    gets[:, 1] = 1
    for (r, c), queue in queues.items():
        turn = (r + c // 2) % len(queue) if (r, c) != (0, 0) else 0
        for step, (form, index, to) in enumerate(queue[turn:] + queue[:turn]):
            moves[step].append((at(r, c), at(*to)))
            sends[at(r, c), step] = form, index
            gets[at(*to)] = step, form
    return moves, sends, gets


def pack_parent_kernel(sends, pattern, own, *outs):
    for step, out in enumerate(outs):
        last = step == len(outs) - 1
        form = 1 if last else sends[step, 0]
        index = 0 if last else sends[step, 1]
        for j in range(NB):
            i, k = (index, j) if last else (
                jnp.where(form == 0, j, index), jnp.where(form == 0, index, j)
            )
            keep = pattern[i, k].astype(F32)
            out[j] = own[block(i), block(k)] * keep


def pack_parent(sends, pattern, own):
    return pl.pallas_call(
        pack_parent_kernel,
        out_shape=(jax.ShapeDtypeStruct((NB, B, B), F32),) * (sends.shape[0] + 1),
        in_specs=[SMEM, SMEM, VMEM],
        out_specs=(VMEM,) * (sends.shape[0] + 1),
        compiler_params=params(60),
        name="pack_parent",
    )(sends, pattern, own)


def pack_small_kernel(ids, cmap, child, small, sems):
    r, c = ids[0], ids[1]
    mine = r // 4 * 4 + c // 4
    ja, _ = find(cmap, mine, c % 4, lambda v: v < 8)
    ia, iv = find(cmap, mine, r % 4, lambda v: v < 8)
    ja = jnp.maximum(ja, 0)
    made = []
    for a in range(8):
        dst = small.at[cmap[mine, r % 4 * 8 + a] // 16, 0]
        made.append(pltpu.make_async_copy(child.at[block(a), block(ja)], dst, sems.at[a]))
    src = child.at[block(jnp.maximum(ia, 0)), block(ja)]
    made.append(pltpu.make_async_copy(src, small.at[jnp.minimum(iv, 7), 1], sems.at[8]))
    for m in made:
        m.start()
    for m in made:
        m.wait()


def pack_small(ids, cmap, child):
    return pl.pallas_call(
        pack_small_kernel,
        out_shape=jax.ShapeDtypeStruct((ROWS, 2, B, B), F32),
        in_specs=[SMEM, SMEM, VMEM],
        out_specs=HBM,
        scratch_shapes=[pltpu.SemaphoreType.DMA((9,))],
        compiler_params=params(12),
        name="pack_small",
    )(ids, cmap, child)


def pack_kernel(ids, cmap, child, bulk, sems):
    r, c = ids[0], ids[1]
    mine = r // 4 * 4 + c // 4

    def copy(n):
        a, b = n // 8, n % 8
        slot = cmap[mine, r % 4 * 8 + a] // 16 * COLS + cmap[mine, c % 4 * 8 + b] // 8
        return pltpu.make_async_copy(child.at[block(a), block(b)], bulk.at[slot], sems.at[n])

    lax.fori_loop(0, 64, lambda n, _: (copy(n).start(), 0)[1], 0)
    lax.fori_loop(0, 64, lambda n, _: (copy(n).wait(), 0)[1], 0)


def pack(ids, cmap, child):
    return pl.pallas_call(
        pack_kernel,
        out_shape=jax.ShapeDtypeStruct((ROWS * COLS, B, B), F32),
        in_specs=[SMEM, SMEM, VMEM],
        out_specs=HBM,
        scratch_shapes=[pltpu.SemaphoreType.DMA((64,))],
        compiler_params=params(60),
        name="pack",
    )(ids, cmap, child)


def relay_kernel(ids, cmap, came, parent, owners, diag, sems):
    r, c = ids[0], ids[1]
    copies = [(parent.at[0], diag.at[2])]
    for half in range(2):
        child = half * 4 + c // 4
        pick = jnp.int32(half * 4)
        for k in range(4):
            src = half * 4 + k
            _, entry = find(cmap, child, k, lambda v: v // 16 == r)
            copies.append((came.at[src, 0], owners.at[entry % 16, half]))
            at, _ = find(cmap, child, k, lambda v: v == r)
            pick = jnp.where(at >= 0, src, pick)
        copies.append((came.at[pick, 1], diag.at[half]))
    made = [pltpu.make_async_copy(s, d, sems.at[n]) for n, (s, d) in enumerate(copies)]
    for m in made:
        m.start()
    for m in made:
        m.wait()


def relay(ids, cmap, came, parent):
    return pl.pallas_call(
        relay_kernel,
        out_shape=(
            jax.ShapeDtypeStruct((COLS, 2, B, B), F32),
            jax.ShapeDtypeStruct((3, B, B), F32),
        ),
        in_specs=[SMEM, SMEM, VMEM, VMEM],
        out_specs=(HBM, HBM),
        scratch_shapes=[pltpu.SemaphoreType.DMA((11,))],
        compiler_params=params(60),
        name="relay",
    )(ids, cmap, came, parent)


def gather_rows(cmap, wanted, came, out):
    for child in range(8):
        half, quarter = child // 4, child % 4
        hit = lax.fori_loop(
            0, 32, lambda n, h: h | (cmap[child, n] == wanted).astype(jnp.int32), jnp.int32(0)
        )

        @pl.when(hit > 0)
        def _():
            for g in range(4):
                at, entry = find(cmap, child, g, lambda v: v < 8)

                @pl.when(at >= 0)
                def _():
                    where = block(jnp.minimum(entry, 7))
                    out[:, where] = out[:, where] + came[quarter * 4 + g, half]


def owner_kernel(ids, cmap, start, came, out):
    @pl.when(ids[2] == 0)
    def _():
        for k in range(NB):
            out[:, k * B : (k + 1) * B] = start[k].T

    @pl.when(ids[2] != 0)
    def _():
        for k in range(NB):
            out[:, k * B : (k + 1) * B] = start[k]

    gather_rows(cmap, ids[0] * COLS + ids[1], came, out)


def owner_rows(ids, cmap, start, came):
    return pl.pallas_call(
        owner_kernel,
        out_shape=jax.ShapeDtypeStruct((B, W), F32),
        in_specs=[SMEM, SMEM, VMEM, VMEM],
        out_specs=VMEM,
        compiler_params=params(24),
        name="owner_rows",
    )(ids, cmap, start, came)


def diag_kernel(ids, cmap, came, out):
    out[:, :B] = came[0, 2].T
    for k in range(1, NB):
        out[:, k * B : (k + 1) * B] = came[k, 2]
    gather_rows(cmap, ids[0], came, out)


def diag_rows(ids, cmap, came):
    return pl.pallas_call(
        diag_kernel,
        out_shape=jax.ShapeDtypeStruct((B, W), F32),
        in_specs=[SMEM, SMEM, VMEM],
        out_specs=VMEM,
        compiler_params=params(24),
        name="diag_rows",
    )(ids, cmap, came)


def spread_lane(x, k):
    return jnp.broadcast_to(x[:, k : k + 1], (8, B))


def spread_sub(x, k):
    return jnp.broadcast_to(x[k : k + 1, :], (8, B))


def eliminate_block(strips):
    sub = lax.broadcasted_iota(jnp.int32, (8, B), 0)
    lane = lax.broadcasted_iota(jnp.int32, (8, B), 1)
    strips = list(strips)
    for m in range(16):
        first = 8 * m
        inside = (lane >= first) & (lane < first + 8)
        w = strips[m]
        cols = [spread_lane(w, first + k) for k in range(8)]
        scales, rows, mults = [], [], []
        for k in range(8):
            rs = lax.rsqrt(spread_sub(cols[k], k))
            row = jnp.where(lane == first + k, rs, spread_sub(w, k) * rs)
            p = cols[k] * rs
            mult = [spread_sub(p, q) for q in range(k + 1, 8)]
            for n, q in enumerate(range(k + 1, 8)):
                cols[q] = cols[q] - p * mult[n]
            rest = jnp.where(lane == first + k, 0.0, w) - p * row
            w = jnp.where(sub > k, rest, jnp.where(sub == k, row, w))
            scales.append(rs)
            rows.append(jnp.where(inside & (lane > first + k), 0.0, row))
            mults.append(mult)
        strips[m] = w
        for s in range(m + 1, 16):
            v = strips[s]
            below = [spread_lane(v, first + k) for k in range(8)]
            v = jnp.where(inside, 0.0, v)
            for k in range(8):
                p = below[k] * scales[k]
                v = v - p * rows[k]
                for n, q in enumerate(range(k + 1, 8)):
                    below[q] = below[q] - p * mults[k][n]
            strips[s] = v
    return strips


def dot32(a, b, ca, cb):
    return lax.dot_general(
        a, b, (((ca,), (cb,)), ((), ())), precision=lax.Precision.HIGHEST, preferred_element_type=F32
    )


def factor_kernel(a_ref, w_ref, d_ref, q_ref):
    row = lax.broadcasted_iota(jnp.int32, (B, B), 0)
    col = lax.broadcasted_iota(jnp.int32, (B, B), 1)
    w_ref[...] = a_ref[...]

    def step(kb, _):
        here = block(kb)
        d_ref[...] = w_ref[here, here]
        strips = eliminate_block([d_ref[8 * s : 8 * s + 8, :] for s in range(16)])
        for s in range(16):
            d_ref[8 * s : 8 * s + 8, :] = strips[s]
        inverse = jnp.where(row >= col, d_ref[...], 0.0)
        q_ref[...] = dot32(inverse, w_ref[here, :], 1, 0)
        q_ref[:, here] = inverse

        def below(i, _):
            rows = block(i)
            w_ref[rows, here] = jnp.zeros((B, B), F32)
            w_ref[rows, :] = w_ref[rows, :] - dot32(q_ref[:, rows], q_ref[...], 0, 0)
            return 0

        lax.fori_loop(kb + 1, NB, below, 0)
        w_ref[here, :] = q_ref[...]
        w_ref[here, here] = d_ref[...]
        return 0

    lax.fori_loop(0, NB, step, 0)


def factor(a):
    return pl.pallas_call(
        factor_kernel,
        out_shape=jax.ShapeDtypeStruct((W, W), F32),
        in_specs=[VMEM],
        out_specs=VMEM,
        scratch_shapes=[pltpu.VMEM((B, B), F32), pltpu.VMEM((B, W), F32)],
        compiler_params=params(32),
        name="factor",
    )(a)


def halves(x):
    high = x.astype(BF16)
    return high, (x - high.astype(F32)).astype(BF16)


def dot_nt(a, b):
    return lax.dot_general(a, b, (((1,), (1,)), ((), ())), preferred_element_type=F32)


def dot3(ah, al, bh, bl):
    return dot_nt(ah, bh) + (dot_nt(ah, bl) + dot_nt(al, bh))


SOLVE = 256
CHUNK = 256


def solve_rows(raw, out, eh, el):
    xh, xl = halves(raw)
    for j in range(W // SOLVE):
        upto = (j + 1) * SOLVE
        rows = slice(j * SOLVE, upto)
        out[:, rows] = dot3(xh[:, :upto], xl[:, :upto], eh[rows, :upto], el[rows, :upto])


def update_kernel(ids, pattern, w_ref, xc_ref, xr_ref, own_ref, out_ref, eh, el, ch, cl, x):
    step = pl.program_id(0)
    r, c = ids[0], ids[1]

    @pl.when(step == 0)
    def _():
        row = lax.broadcasted_iota(jnp.int32, (B, W), 0)
        col = lax.broadcasted_iota(jnp.int32, (B, W), 1)

        def split(i, _):
            rows = block(i)
            high, low = halves(jnp.where(row + i * B >= col, w_ref[rows, :], 0.0))
            eh[rows, :] = high
            el[rows, :] = low
            return 0

        lax.fori_loop(0, NB, split, 0)

        def columns(i, _):
            rows = pl.ds(pl.multiple_of(i * CHUNK, CHUNK), CHUNK)
            solve_rows(xc_ref[rows, :], x, eh, el)
            high, low = halves(x[...])
            ch[rows, :] = high
            cl[rows, :] = low
            return 0

        lax.fori_loop(0, W // CHUNK, columns, 0)

    solve_rows(xr_ref[...], x, eh, el)
    top = (r == 0) & (step < W // CHUNK)

    @pl.when((c > 0) & top)
    def _():
        out_ref[...] = jnp.zeros_like(out_ref)

    @pl.when((c > 0) & jnp.logical_not(top))
    def _():
        high, low = halves(x[...])
        for j in range(W // SOLVE):
            cols = slice(j * SOLVE, (j + 1) * SOLVE)
            change = dot3(high, low, ch[cols, :], cl[cols, :])
            for a in range(CHUNK // B):
                for b in range(SOLVE // B):
                    rs = slice(a * B, (a + 1) * B)
                    k = j * (SOLVE // B) + b
                    cs = slice(k * B, (k + 1) * B)
                    keep = pattern[step * (CHUNK // B) + a, k].astype(F32)
                    out_ref[rs, cs] = own_ref[rs, cs] * keep - change[rs, b * B : (b + 1) * B]

    @pl.when((c == 0) & jnp.logical_not(top))
    def _():
        out_ref[...] = x[...]

    @pl.when((c == 0) & top)
    def _():
        row = lax.broadcasted_iota(jnp.int32, (CHUNK, B), 0)
        col = lax.broadcasted_iota(jnp.int32, (CHUNK, B), 1)
        for j in range(NB):
            cols = slice(j * B, (j + 1) * B)
            rows = pl.ds(pl.multiple_of(step * CHUNK, CHUNK), CHUNK)
            above = w_ref[cols, rows].T
            here = w_ref[rows, cols]
            gap = row + step * CHUNK - (col + j * B)
            out_ref[:, cols] = jnp.where(gap > 0, above, jnp.where(gap == 0, 1.0 / here, 0.0))


def update(ids, pattern, w, xc, xr, own):
    rows = own.shape[0]
    whole = pl.BlockSpec((W, W), lambda i: (0, 0), pipeline_mode=pl.Buffered(1))
    part = pl.BlockSpec((CHUNK, W), lambda i: (i, 0))
    return pl.pallas_call(
        update_kernel,
        grid=(rows // CHUNK,),
        out_shape=jax.ShapeDtypeStruct(own.shape, F32),
        in_specs=[SMEM, SMEM, whole, whole, part, part],
        out_specs=part,
        scratch_shapes=[pltpu.VMEM((W, W), BF16)] * 4 + [pltpu.VMEM((CHUNK, W), F32)],
        compiler_params=params(60),
        name="update",
    )(ids, pattern, w, xc, xr, own)


def add_kernel(places, base, came, out, held, sems):
    step = pl.program_id(0)

    def visit(group, act):
        def one(quarter, _):
            child = group // 4
            slot = (child // 4 * 4 + group % 4) * COLS + child % 4 * 4 + quarter
            col = places[1, child * 4 + quarter]

            @pl.when(col >= 0)
            def _():
                act(pltpu.make_async_copy(came.at[slot], held.at[slot], sems.at[slot]), slot, col)

            return 0

        lax.fori_loop(0, 4, one, 0)

    @pl.when(step == 0)
    def _():
        def begin(group, _):
            @pl.when(places[0, group] >= 0)
            def _():
                visit(group, lambda m, slot, col: m.start())

            return 0

        lax.fori_loop(0, 32, begin, 0)

    out[...] = base[...]

    def finish(group, _):
        row = places[0, group]

        def act(m, slot, col):
            m.wait()
            here = block(row % (CHUNK // B)), block(col)
            out[here] = out[here] + held[slot]

        @pl.when((row >= 0) & (row // (CHUNK // B) == step))
        def _():
            visit(group, act)

        return 0

    lax.fori_loop(0, 32, finish, 0)


def add(places, base, came):
    part = pl.BlockSpec((CHUNK, W), lambda i: (i, 0))
    return pl.pallas_call(
        add_kernel,
        grid=(base.shape[0] // CHUNK,),
        out_shape=jax.ShapeDtypeStruct(base.shape, F32),
        in_specs=[SMEM, part, HBM],
        out_specs=part,
        scratch_shapes=[
            pltpu.VMEM((ROWS * COLS, B, B), F32),
            pltpu.SemaphoreType.DMA((ROWS * COLS,)),
        ],
        compiler_params=params(60),
        name="add",
    )(places, base, came)


def at(r, c):
    return r * COLS + c


def after(value, first):
    return lax.optimization_barrier((value, first))[0]


def body(child, own, pattern, cmap):
    row, col = lax.axis_index("prow"), lax.axis_index("pcol")
    moves, sends, gets = scatter_plan()
    mine = lax.dynamic_index_in_dim(jnp.asarray(gets), at(row, col), 0, keepdims=False)
    ids = jnp.stack([row, col, mine[1]]).astype(jnp.int32)
    sends = lax.dynamic_index_in_dim(jnp.asarray(sends), at(row, col), 0, keepdims=False)

    places = cmap.reshape(32, 8)
    low, high = places % 16, places % 8
    rok = (places // 16 == row) & ((row > 0) | (low >= 8))
    cok = (places // 8 == col) & (col > 0)
    places = jnp.stack(
        [jnp.max(jnp.where(rok, low, -1), axis=1), jnp.max(jnp.where(cok, high, -1), axis=1)]
    )

    *pieces, start = pack_parent(sends, pattern, own)
    small = pack_small(ids, cmap, child)
    small = lax.all_to_all(small, "prow", 0, 0, tiled=True)
    for step, piece in enumerate(pieces):
        piece = lax.ppermute(piece, AXES, moves[step])
        start = jnp.where(mine[0] == step, piece, start)
    parent = lax.all_to_all(start, "prow", 0, 0, tiled=True)

    owners, diag = relay(ids, cmap, small, parent)
    diag = lax.all_gather(diag, "pcol", axis=0)
    owners = lax.all_to_all(owners, "pcol", 0, 0, tiled=True)
    owned = owner_rows(ids, cmap, start, owners)
    to = [(at(r, c), at(c % 8, 2 * r + c // 8)) for r in range(ROWS) for c in range(COLS)]
    xc = lax.ppermute(owned, AXES, to)

    bulk = after(pack(ids, cmap, child), owners)
    bulk = lax.all_to_all(bulk, AXES, 0, 0, tiled=True)

    pivot = diag_rows(ids, cmap, after(diag, xc))
    pivot = lax.all_gather(pivot, "prow", axis=0, tiled=True)
    xr = lax.all_gather(owned, "pcol", axis=0, tiled=True)
    xc = lax.all_gather(xc, "prow", axis=0, tiled=True)
    w = factor(pivot)
    base = update(ids, pattern, w, xc, xr, own)
    return add(places, base, bulk)


def solution(mesh):
    return jax.shard_map(
        body,
        mesh=mesh,
        in_specs=(P("prow", "pcol"), P("prow", "pcol"), P("prow", "pcol"), P()),
        out_specs=P("prow", "pcol"),
        check_vma=False,
    )
```

```python
import jax
import jax.numpy as jnp
import numpy as np
from jax import lax
from jax.experimental import pallas as pl
from jax.experimental.pallas import tpu as pltpu
from jax.sharding import PartitionSpec as P

B = 128
NB = 8
W = B * NB
ROWS = 8
COLS = 16
AXES = ("prow", "pcol")
F32 = jnp.float32
BF16 = jnp.bfloat16
HBM = pl.BlockSpec(memory_space=pltpu.HBM)
SMEM = pl.BlockSpec(memory_space=pltpu.SMEM)
VMEM = pl.BlockSpec(memory_space=pltpu.VMEM)
MIB = 1024 * 1024


def params(mib):
    return pltpu.CompilerParams(vmem_limit_bytes=mib * MIB)


def block(at):
    return pl.ds(pl.multiple_of(at * B, B), B)


def find(cmap, child, group, test):
    at = jnp.int32(-1)
    entry = jnp.int32(0)
    for k in range(8):
        value = cmap[child, group * 8 + k]
        hit = test(value)
        at = jnp.where(hit, k, at)
        entry = jnp.where(hit, value, entry)
    return at, entry


def scatter_plan():
    queues = {}
    for r in range(ROWS):
        for c in range(1, COLS):
            if r == 0:
                move = ((0, c // 8), 0, c % 8)
            elif c % 8 < 5:
                move = ((0, 2 * r + c // 8), 0, c % 8)
            else:
                move = ((r, 0), 1, c)
            queues.setdefault(move[0], []).append((move[1], move[2], (r, c)))
    steps = max(len(q) for q in queues.values())
    moves = [[] for _ in range(steps)]
    sends = np.zeros((ROWS * COLS, steps, 2), np.int32)
    gets = np.zeros((ROWS * COLS, 2), np.int32)
    gets[:, 0] = -1
    gets[:, 1] = 1
    for (r, c), queue in queues.items():
        turn = (r + c // 2) % len(queue) if (r, c) != (0, 0) else 0
        for step, (form, index, to) in enumerate(queue[turn:] + queue[:turn]):
            moves[step].append((at(r, c), at(*to)))
            sends[at(r, c), step] = form, index
            gets[at(*to)] = step, form
    return moves, sends, gets


def pack_parent_kernel(sends, pattern, own, *outs):
    for step, out in enumerate(outs):
        last = step == len(outs) - 1
        form = 1 if last else sends[step, 0]
        index = 0 if last else sends[step, 1]
        for j in range(NB):
            i, k = (index, j) if last else (
                jnp.where(form == 0, j, index), jnp.where(form == 0, index, j)
            )
            keep = pattern[i, k].astype(F32)
            out[j] = own[block(i), block(k)] * keep


def pack_parent(sends, pattern, own):
    return pl.pallas_call(
        pack_parent_kernel,
        out_shape=(jax.ShapeDtypeStruct((NB, B, B), F32),) * (sends.shape[0] + 1),
        in_specs=[SMEM, SMEM, VMEM],
        out_specs=(VMEM,) * (sends.shape[0] + 1),
        compiler_params=params(60),
        name="pack_parent",
    )(sends, pattern, own)


def pack_small_kernel(ids, cmap, child, small, sems):
    r, c = ids[0], ids[1]
    mine = r // 4 * 4 + c // 4
    ja, _ = find(cmap, mine, c % 4, lambda v: v < 8)
    ia, iv = find(cmap, mine, r % 4, lambda v: v < 8)
    ja = jnp.maximum(ja, 0)
    made = []
    for a in range(8):
        dst = small.at[cmap[mine, r % 4 * 8 + a] // 16, 0]
        made.append(pltpu.make_async_copy(child.at[block(a), block(ja)], dst, sems.at[a]))
    src = child.at[block(jnp.maximum(ia, 0)), block(ja)]
    made.append(pltpu.make_async_copy(src, small.at[jnp.minimum(iv, 7), 1], sems.at[8]))
    for m in made:
        m.start()
    for m in made:
        m.wait()


def pack_small(ids, cmap, child):
    return pl.pallas_call(
        pack_small_kernel,
        out_shape=jax.ShapeDtypeStruct((ROWS, 2, B, B), F32),
        in_specs=[SMEM, SMEM, VMEM],
        out_specs=HBM,
        scratch_shapes=[pltpu.SemaphoreType.DMA((9,))],
        compiler_params=params(12),
        name="pack_small",
    )(ids, cmap, child)


def pack_kernel(ids, cmap, child, bulk, sems):
    r, c = ids[0], ids[1]
    mine = r // 4 * 4 + c // 4

    def copy(n):
        a, b = n // 8, n % 8
        slot = cmap[mine, r % 4 * 8 + a] // 16 * COLS + cmap[mine, c % 4 * 8 + b] // 8
        return pltpu.make_async_copy(child.at[block(a), block(b)], bulk.at[slot], sems.at[n])

    lax.fori_loop(0, 64, lambda n, _: (copy(n).start(), 0)[1], 0)
    lax.fori_loop(0, 64, lambda n, _: (copy(n).wait(), 0)[1], 0)


def pack(ids, cmap, child):
    return pl.pallas_call(
        pack_kernel,
        out_shape=jax.ShapeDtypeStruct((ROWS * COLS, B, B), F32),
        in_specs=[SMEM, SMEM, VMEM],
        out_specs=HBM,
        scratch_shapes=[pltpu.SemaphoreType.DMA((64,))],
        compiler_params=params(60),
        name="pack",
    )(ids, cmap, child)


def relay_kernel(ids, cmap, came, parent, owners, diag, sems):
    r, c = ids[0], ids[1]
    copies = [(parent.at[0], diag.at[2])]
    for half in range(2):
        child = half * 4 + c // 4
        pick = jnp.int32(half * 4)
        for k in range(4):
            src = half * 4 + k
            _, entry = find(cmap, child, k, lambda v: v // 16 == r)
            copies.append((came.at[src, 0], owners.at[entry % 16, half]))
            at, _ = find(cmap, child, k, lambda v: v == r)
            pick = jnp.where(at >= 0, src, pick)
        copies.append((came.at[pick, 1], diag.at[half]))
    made = [pltpu.make_async_copy(s, d, sems.at[n]) for n, (s, d) in enumerate(copies)]
    for m in made:
        m.start()
    for m in made:
        m.wait()


def relay(ids, cmap, came, parent):
    return pl.pallas_call(
        relay_kernel,
        out_shape=(
            jax.ShapeDtypeStruct((COLS, 2, B, B), F32),
            jax.ShapeDtypeStruct((3, B, B), F32),
        ),
        in_specs=[SMEM, SMEM, VMEM, VMEM],
        out_specs=(HBM, HBM),
        scratch_shapes=[pltpu.SemaphoreType.DMA((11,))],
        compiler_params=params(60),
        name="relay",
    )(ids, cmap, came, parent)


def gather_rows(cmap, wanted, came, out):
    for child in range(8):
        half, quarter = child // 4, child % 4
        hit = lax.fori_loop(
            0, 32, lambda n, h: h | (cmap[child, n] == wanted).astype(jnp.int32), jnp.int32(0)
        )

        @pl.when(hit > 0)
        def _():
            for g in range(4):
                at, entry = find(cmap, child, g, lambda v: v < 8)

                @pl.when(at >= 0)
                def _():
                    where = block(jnp.minimum(entry, 7))
                    out[:, where] = out[:, where] + came[quarter * 4 + g, half]


def owner_kernel(ids, cmap, start, came, out):
    @pl.when(ids[2] == 0)
    def _():
        for k in range(NB):
            out[:, k * B : (k + 1) * B] = start[k].T

    @pl.when(ids[2] != 0)
    def _():
        for k in range(NB):
            out[:, k * B : (k + 1) * B] = start[k]

    gather_rows(cmap, ids[0] * COLS + ids[1], came, out)


def owner_rows(ids, cmap, start, came):
    return pl.pallas_call(
        owner_kernel,
        out_shape=jax.ShapeDtypeStruct((B, W), F32),
        in_specs=[SMEM, SMEM, VMEM, VMEM],
        out_specs=VMEM,
        compiler_params=params(24),
        name="owner_rows",
    )(ids, cmap, start, came)


def diag_kernel(ids, cmap, came, out):
    out[:, :B] = came[0, 2].T
    for k in range(1, NB):
        out[:, k * B : (k + 1) * B] = came[k, 2]
    gather_rows(cmap, ids[0], came, out)


def diag_rows(ids, cmap, came):
    return pl.pallas_call(
        diag_kernel,
        out_shape=jax.ShapeDtypeStruct((B, W), F32),
        in_specs=[SMEM, SMEM, VMEM],
        out_specs=VMEM,
        compiler_params=params(24),
        name="diag_rows",
    )(ids, cmap, came)


def spread_lane(x, k):
    return jnp.broadcast_to(x[:, k : k + 1], (8, B))


def spread_sub(x, k):
    return jnp.broadcast_to(x[k : k + 1, :], (8, B))


def eliminate_block(strips):
    sub = lax.broadcasted_iota(jnp.int32, (8, B), 0)
    lane = lax.broadcasted_iota(jnp.int32, (8, B), 1)
    strips = list(strips)
    for m in range(16):
        first = 8 * m
        inside = (lane >= first) & (lane < first + 8)
        w = strips[m]
        cols = [spread_lane(w, first + k) for k in range(8)]
        scales, rows, mults = [], [], []
        for k in range(8):
            rs = lax.rsqrt(spread_sub(cols[k], k))
            row = jnp.where(lane == first + k, rs, spread_sub(w, k) * rs)
            p = cols[k] * rs
            mult = [spread_sub(p, q) for q in range(k + 1, 8)]
            for n, q in enumerate(range(k + 1, 8)):
                cols[q] = cols[q] - p * mult[n]
            rest = jnp.where(lane == first + k, 0.0, w) - p * row
            w = jnp.where(sub > k, rest, jnp.where(sub == k, row, w))
            scales.append(rs)
            rows.append(jnp.where(inside & (lane > first + k), 0.0, row))
            mults.append(mult)
        strips[m] = w
        for s in range(m + 1, 16):
            v = strips[s]
            below = [spread_lane(v, first + k) for k in range(8)]
            v = jnp.where(inside, 0.0, v)
            for k in range(8):
                p = below[k] * scales[k]
                v = v - p * rows[k]
                for n, q in enumerate(range(k + 1, 8)):
                    below[q] = below[q] - p * mults[k][n]
            strips[s] = v
    return strips


def dot32(a, b, ca, cb):
    return lax.dot_general(
        a, b, (((ca,), (cb,)), ((), ())), precision=lax.Precision.HIGHEST, preferred_element_type=F32
    )


def piece_rows(r):
    rows = []
    for d in range(ROWS // 2):
        x = (r // 2 + ROWS // 2 - d) % (ROWS // 2)
        rows += [2 * x + r % 2, 2 * x + 1 - r % 2]
    return rows


def factor_kernel(ids, *refs):
    pieces, (w_ref, d_ref, q_ref) = refs[:ROWS], refs[ROWS:]
    row = lax.broadcasted_iota(jnp.int32, (B, B), 0)
    col = lax.broadcasted_iota(jnp.int32, (B, B), 1)
    for k, piece in zip(piece_rows(ids[0]), pieces):
        w_ref[block(k), :] = piece[...]

    def step(kb, _):
        here = block(kb)
        d_ref[...] = w_ref[here, here]
        strips = eliminate_block([d_ref[8 * s : 8 * s + 8, :] for s in range(16)])
        for s in range(16):
            d_ref[8 * s : 8 * s + 8, :] = strips[s]
        inverse = jnp.where(row >= col, d_ref[...], 0.0)
        q_ref[...] = dot32(inverse, w_ref[here, :], 1, 0)
        q_ref[:, here] = inverse

        def below(i, _):
            rows = block(i)
            w_ref[rows, here] = jnp.zeros((B, B), F32)
            w_ref[rows, :] = w_ref[rows, :] - dot32(q_ref[:, rows], q_ref[...], 0, 0)
            return 0

        lax.fori_loop(kb + 1, NB, below, 0)
        w_ref[here, :] = q_ref[...]
        w_ref[here, here] = d_ref[...]
        return 0

    lax.fori_loop(0, NB, step, 0)


def factor(ids, pieces):
    return pl.pallas_call(
        factor_kernel,
        out_shape=jax.ShapeDtypeStruct((W, W), F32),
        in_specs=[SMEM] + [VMEM] * ROWS,
        out_specs=VMEM,
        scratch_shapes=[pltpu.VMEM((B, B), F32), pltpu.VMEM((B, W), F32)],
        compiler_params=params(32),
        name="factor",
    )(ids, *pieces)


def halves(x):
    high = x.astype(BF16)
    return high, (x - high.astype(F32)).astype(BF16)


def dot_nt(a, b):
    return lax.dot_general(a, b, (((1,), (1,)), ((), ())), preferred_element_type=F32)


def dot3(ah, al, bh, bl):
    return dot_nt(ah, bh) + (dot_nt(ah, bl) + dot_nt(al, bh))


SOLVE = 256
CHUNK = 256


def solve_rows(raw, out, eh, el):
    xh, xl = halves(raw)
    for j in range(W // SOLVE):
        upto = (j + 1) * SOLVE
        rows = slice(j * SOLVE, upto)
        out[:, rows] = dot3(xh[:, :upto], xl[:, :upto], eh[rows, :upto], el[rows, :upto])


def update_kernel(ids, pattern, w_ref, *refs):
    pieces, (xr_ref, own_ref, out_ref, eh, el, ch, cl, x) = refs[:ROWS], refs[ROWS:]
    step = pl.program_id(0)
    r, c = ids[0], ids[1]

    @pl.when(step == 0)
    def _():
        row = lax.broadcasted_iota(jnp.int32, (B, W), 0)
        col = lax.broadcasted_iota(jnp.int32, (B, W), 1)

        def split(i, _):
            rows = block(i)
            high, low = halves(jnp.where(row + i * B >= col, w_ref[rows, :], 0.0))
            eh[rows, :] = high
            el[rows, :] = low
            return 0

        lax.fori_loop(0, NB, split, 0)

        at_row = piece_rows(r)
        for n in range(0, ROWS, 2):
            pair = jnp.concatenate([pieces[n][...], pieces[n + 1][...]], axis=0)
            solve_rows(pair, x, eh, el)
            for m in range(2):
                high, low = halves(x[m * B : (m + 1) * B, :])
                ch[block(at_row[n + m]), :] = high
                cl[block(at_row[n + m]), :] = low

    solve_rows(xr_ref[...], x, eh, el)
    top = (r == 0) & (step < W // CHUNK)

    @pl.when((c > 0) & top)
    def _():
        out_ref[...] = jnp.zeros_like(out_ref)

    @pl.when((c > 0) & jnp.logical_not(top))
    def _():
        high, low = halves(x[...])
        for j in range(W // SOLVE):
            cols = slice(j * SOLVE, (j + 1) * SOLVE)
            change = dot3(high, low, ch[cols, :], cl[cols, :])
            for a in range(CHUNK // B):
                for b in range(SOLVE // B):
                    rs = slice(a * B, (a + 1) * B)
                    k = j * (SOLVE // B) + b
                    cs = slice(k * B, (k + 1) * B)
                    keep = pattern[step * (CHUNK // B) + a, k].astype(F32)
                    out_ref[rs, cs] = own_ref[rs, cs] * keep - change[rs, b * B : (b + 1) * B]

    @pl.when((c == 0) & jnp.logical_not(top))
    def _():
        out_ref[...] = x[...]

    @pl.when((c == 0) & top)
    def _():
        row = lax.broadcasted_iota(jnp.int32, (CHUNK, B), 0)
        col = lax.broadcasted_iota(jnp.int32, (CHUNK, B), 1)
        for j in range(NB):
            cols = slice(j * B, (j + 1) * B)
            rows = pl.ds(pl.multiple_of(step * CHUNK, CHUNK), CHUNK)
            above = w_ref[cols, rows].T
            here = w_ref[rows, cols]
            gap = row + step * CHUNK - (col + j * B)
            out_ref[:, cols] = jnp.where(gap > 0, above, jnp.where(gap == 0, 1.0 / here, 0.0))


def update(ids, pattern, w, xc, xr, own):
    rows = own.shape[0]
    whole = pl.BlockSpec((W, W), lambda i: (0, 0), pipeline_mode=pl.Buffered(1))
    piece = pl.BlockSpec((B, W), lambda i: (0, 0), pipeline_mode=pl.Buffered(1))
    part = pl.BlockSpec((CHUNK, W), lambda i: (i, 0))
    return pl.pallas_call(
        update_kernel,
        grid=(rows // CHUNK,),
        out_shape=jax.ShapeDtypeStruct(own.shape, F32),
        in_specs=[SMEM, SMEM, whole] + [piece] * ROWS + [part, part],
        out_specs=part,
        scratch_shapes=[pltpu.VMEM((W, W), BF16)] * 4 + [pltpu.VMEM((CHUNK, W), F32)],
        compiler_params=params(60),
        name="update",
    )(ids, pattern, w, *xc, xr, own)


def add_kernel(places, base, came, out, held, sems):
    step = pl.program_id(0)

    def visit(group, act):
        def one(quarter, _):
            child = group // 4
            slot = (child // 4 * 4 + group % 4) * COLS + child % 4 * 4 + quarter
            col = places[1, child * 4 + quarter]

            @pl.when(col >= 0)
            def _():
                act(pltpu.make_async_copy(came.at[slot], held.at[slot], sems.at[slot]), slot, col)

            return 0

        lax.fori_loop(0, 4, one, 0)

    @pl.when(step == 0)
    def _():
        def begin(group, _):
            @pl.when(places[0, group] >= 0)
            def _():
                visit(group, lambda m, slot, col: m.start())

            return 0

        lax.fori_loop(0, 32, begin, 0)

    out[...] = base[...]

    def finish(group, _):
        row = places[0, group]

        def act(m, slot, col):
            m.wait()
            here = block(row % (CHUNK // B)), block(col)
            out[here] = out[here] + held[slot]

        @pl.when((row >= 0) & (row // (CHUNK // B) == step))
        def _():
            visit(group, act)

        return 0

    lax.fori_loop(0, 32, finish, 0)


def add(places, base, came):
    part = pl.BlockSpec((CHUNK, W), lambda i: (i, 0))
    return pl.pallas_call(
        add_kernel,
        grid=(base.shape[0] // CHUNK,),
        out_shape=jax.ShapeDtypeStruct(base.shape, F32),
        in_specs=[SMEM, part, HBM],
        out_specs=part,
        scratch_shapes=[
            pltpu.VMEM((ROWS * COLS, B, B), F32),
            pltpu.SemaphoreType.DMA((ROWS * COLS,)),
        ],
        compiler_params=params(60),
        name="add",
    )(places, base, came)


def at(r, c):
    return r * COLS + c


def after(value, first):
    return lax.optimization_barrier((value, first))[0]


def along_x(piece):
    half = ROWS // 2
    pieces = [piece]
    for d in range(1, half):
        to = [(2 * x + k, 2 * ((x + d) % half) + k) for x in range(half) for k in range(2)]
        pieces.append(lax.ppermute(piece, "prow", to))
    return pieces


def across(pieces):
    both = []
    for piece in pieces:
        both += [piece, lax.ppermute(piece, "prow", [(k, k ^ 1) for k in range(ROWS)])]
    return both


def body(child, own, pattern, cmap):
    row, col = lax.axis_index("prow"), lax.axis_index("pcol")
    moves, sends, gets = scatter_plan()
    mine = lax.dynamic_index_in_dim(jnp.asarray(gets), at(row, col), 0, keepdims=False)
    ids = jnp.stack([row, col, mine[1]]).astype(jnp.int32)
    sends = lax.dynamic_index_in_dim(jnp.asarray(sends), at(row, col), 0, keepdims=False)

    places = cmap.reshape(32, 8)
    low, high = places % 16, places % 8
    rok = (places // 16 == row) & ((row > 0) | (low >= 8))
    cok = (places // 8 == col) & (col > 0)
    places = jnp.stack(
        [jnp.max(jnp.where(rok, low, -1), axis=1), jnp.max(jnp.where(cok, high, -1), axis=1)]
    )

    *pieces, start = pack_parent(sends, pattern, own)
    small = pack_small(ids, cmap, child)
    small = lax.all_to_all(small, "prow", 0, 0, tiled=True)
    top = start
    for step, piece in enumerate(pieces):
        piece = lax.ppermute(piece, AXES, moves[step])
        start = jnp.where(mine[0] == step, piece, start)
        top = start if step == NB - 2 else top
    parent = lax.all_to_all(top, "prow", 0, 0, tiled=True)

    owners, diag = relay(ids, cmap, small, parent)
    diag = lax.all_gather(diag, "pcol", axis=0)
    diag = diag_rows(ids, cmap, diag)
    pivot = across(along_x(diag))
    owners = lax.all_to_all(after(owners, diag), "pcol", 0, 0, tiled=True)
    owned = owner_rows(ids, cmap, start, after(owners, pivot[2::2]))
    xr = lax.all_gather(owned, "pcol", axis=0, tiled=True)
    to = [(at(r, c), at(c % 8, 2 * r + c // 8)) for r in range(ROWS) for c in range(COLS)]
    xc = lax.ppermute(owned, AXES, to)
    bulk = after(pack(ids, cmap, child), (xc, pivot))
    bulk = lax.all_to_all(bulk, AXES, 0, 0, tiled=True)
    xc = along_x(xc)
    w = factor(ids, pivot)
    xc = across(after(xc, w))
    base = update(ids, pattern, w, xc, xr, own)
    return add(places, base, bulk)


def solution(mesh):
    return jax.shard_map(
        body,
        mesh=mesh,
        in_specs=(P("prow", "pcol"), P("prow", "pcol"), P("prow", "pcol"), P()),
        out_specs=P("prow", "pcol"),
        check_vma=False,
    )
```

```python
import jax
import jax.numpy as jnp
import numpy as np
from jax import lax
from jax.experimental import pallas as pl
from jax.experimental.pallas import tpu as pltpu
from jax.sharding import PartitionSpec as P

B = 128
NB = 8
W = B * NB
ROWS = 8
COLS = 16
AXES = ("prow", "pcol")
F32 = jnp.float32
BF16 = jnp.bfloat16
HBM = pl.BlockSpec(memory_space=pltpu.HBM)
SMEM = pl.BlockSpec(memory_space=pltpu.SMEM)
VMEM = pl.BlockSpec(memory_space=pltpu.VMEM)
MIB = 1024 * 1024
PARTS = 2
PART = B // PARTS


def params(mib):
    return pltpu.CompilerParams(vmem_limit_bytes=mib * MIB)


def block(at):
    return pl.ds(pl.multiple_of(at * B, B), B)


def find(cmap, child, group, test):
    at = jnp.int32(-1)
    entry = jnp.int32(0)
    for k in range(8):
        value = cmap[child, group * 8 + k]
        hit = test(value)
        at = jnp.where(hit, k, at)
        entry = jnp.where(hit, value, entry)
    return at, entry


def scatter_plan():
    queues = {}
    for r in range(ROWS):
        for c in range(1, COLS):
            if r == 0:
                move = ((0, c // 8), 0, c % 8)
            elif c % 8 < 5:
                move = ((0, 2 * r + c // 8), 0, c % 8)
            else:
                move = ((r, 0), 1, c)
            queues.setdefault(move[0], []).append((move[1], move[2], (r, c)))
    steps = max(len(q) for q in queues.values())
    moves = [[] for _ in range(steps)]
    sends = np.zeros((ROWS * COLS, steps, 2), np.int32)
    gets = np.zeros((ROWS * COLS, 2), np.int32)
    gets[:, 0] = -1
    gets[:, 1] = 1
    for (r, c), queue in queues.items():
        turn = (r + c // 2) % len(queue) if (r, c) != (0, 0) else 0
        for step, (form, index, to) in enumerate(queue[turn:] + queue[:turn]):
            moves[step].append((at(r, c), at(*to)))
            sends[at(r, c), step] = form, index
            gets[at(*to)] = step, form
    return moves, sends, gets


def pack_parent_kernel(sends, pattern, own, *outs):
    for step, out in enumerate(outs):
        last = step == len(outs) - 1
        form = 1 if last else sends[step, 0]
        index = 0 if last else sends[step, 1]
        for j in range(NB):
            i, k = (index, j) if last else (
                jnp.where(form == 0, j, index), jnp.where(form == 0, index, j)
            )
            keep = pattern[i, k].astype(F32)
            out[j] = own[block(i), block(k)] * keep


def pack_parent(sends, pattern, own):
    return pl.pallas_call(
        pack_parent_kernel,
        out_shape=(jax.ShapeDtypeStruct((NB, B, B), F32),) * (sends.shape[0] + 1),
        in_specs=[SMEM, SMEM, VMEM],
        out_specs=(VMEM,) * (sends.shape[0] + 1),
        compiler_params=params(60),
        name="pack_parent",
    )(sends, pattern, own)


def pack_small_kernel(ids, cmap, child, small, sems):
    r, c = ids[0], ids[1]
    mine = r // 4 * 4 + c // 4
    ja, _ = find(cmap, mine, c % 4, lambda v: v < 8)
    ia, iv = find(cmap, mine, r % 4, lambda v: v < 8)
    ja = jnp.maximum(ja, 0)
    made = []
    for a in range(8):
        dst = small.at[cmap[mine, r % 4 * 8 + a] // 16, 0]
        made.append(pltpu.make_async_copy(child.at[block(a), block(ja)], dst, sems.at[a]))
    src = child.at[block(jnp.maximum(ia, 0)), block(ja)]
    made.append(pltpu.make_async_copy(src, small.at[jnp.minimum(iv, 7), 1], sems.at[8]))
    for m in made:
        m.start()
    for m in made:
        m.wait()


def pack_small(ids, cmap, child):
    return pl.pallas_call(
        pack_small_kernel,
        out_shape=jax.ShapeDtypeStruct((ROWS, 2, B, B), F32),
        in_specs=[SMEM, SMEM, VMEM],
        out_specs=HBM,
        scratch_shapes=[pltpu.SemaphoreType.DMA((9,))],
        compiler_params=params(12),
        name="pack_small",
    )(ids, cmap, child)


def pack_kernel(ids, cmap, child, *rest):
    bulk, sems = rest[:PARTS], rest[PARTS]
    r, c = ids[0], ids[1]
    mine = r // 4 * 4 + c // 4

    def copies(n):
        a, b = n // 8, n % 8
        slot = cmap[mine, r % 4 * 8 + a] // 16 * COLS + cmap[mine, c % 4 * 8 + b] // 8
        for part in range(PARTS):
            rows = pl.ds(pl.multiple_of(a * B + part * PART, PART), PART)
            src = child.at[rows, block(b)]
            yield pltpu.make_async_copy(src, bulk[part].at[slot], sems.at[n, part])

    def start(n, _):
        for m in copies(n):
            m.start()
        return 0

    def wait(n, _):
        for m in copies(n):
            m.wait()
        return 0

    lax.fori_loop(0, 64, start, 0)
    lax.fori_loop(0, 64, wait, 0)


def pack(ids, cmap, child):
    return pl.pallas_call(
        pack_kernel,
        out_shape=(jax.ShapeDtypeStruct((ROWS * COLS, PART, B), F32),) * PARTS,
        in_specs=[SMEM, SMEM, VMEM],
        out_specs=(HBM,) * PARTS,
        scratch_shapes=[pltpu.SemaphoreType.DMA((64, PARTS))],
        compiler_params=params(60),
        name="pack",
    )(ids, cmap, child)


def relay_kernel(ids, cmap, came, parent, owners, diag, sems):
    r, c = ids[0], ids[1]
    copies = [(parent.at[0], diag.at[2])]
    for half in range(2):
        child = half * 4 + c // 4
        pick = jnp.int32(half * 4)
        for k in range(4):
            src = half * 4 + k
            _, entry = find(cmap, child, k, lambda v: v // 16 == r)
            copies.append((came.at[src, 0], owners.at[entry % 16, half]))
            at, _ = find(cmap, child, k, lambda v: v == r)
            pick = jnp.where(at >= 0, src, pick)
        copies.append((came.at[pick, 1], diag.at[half]))
    made = [pltpu.make_async_copy(s, d, sems.at[n]) for n, (s, d) in enumerate(copies)]
    for m in made:
        m.start()
    for m in made:
        m.wait()


def relay(ids, cmap, came, parent):
    return pl.pallas_call(
        relay_kernel,
        out_shape=(
            jax.ShapeDtypeStruct((COLS, 2, B, B), F32),
            jax.ShapeDtypeStruct((3, B, B), F32),
        ),
        in_specs=[SMEM, SMEM, VMEM, VMEM],
        out_specs=(HBM, HBM),
        scratch_shapes=[pltpu.SemaphoreType.DMA((11,))],
        compiler_params=params(60),
        name="relay",
    )(ids, cmap, came, parent)


def gather_rows(cmap, wanted, came, out):
    for child in range(8):
        half, quarter = child // 4, child % 4
        hit = lax.fori_loop(
            0, 32, lambda n, h: h | (cmap[child, n] == wanted).astype(jnp.int32), jnp.int32(0)
        )

        @pl.when(hit > 0)
        def _():
            for g in range(4):
                at, entry = find(cmap, child, g, lambda v: v < 8)

                @pl.when(at >= 0)
                def _():
                    where = block(jnp.minimum(entry, 7))
                    out[:, where] = out[:, where] + came[quarter * 4 + g, half]


def owner_kernel(ids, cmap, start, came, out):
    @pl.when(ids[2] == 0)
    def _():
        for k in range(NB):
            out[:, k * B : (k + 1) * B] = start[k].T

    @pl.when(ids[2] != 0)
    def _():
        for k in range(NB):
            out[:, k * B : (k + 1) * B] = start[k]

    gather_rows(cmap, ids[0] * COLS + ids[1], came, out)


def owner_rows(ids, cmap, start, came):
    return pl.pallas_call(
        owner_kernel,
        out_shape=jax.ShapeDtypeStruct((B, W), F32),
        in_specs=[SMEM, SMEM, VMEM, VMEM],
        out_specs=VMEM,
        compiler_params=params(24),
        name="owner_rows",
    )(ids, cmap, start, came)


def diag_kernel(ids, cmap, came, out):
    out[:, :B] = came[0, 2].T
    for k in range(1, NB):
        out[:, k * B : (k + 1) * B] = came[k, 2]
    gather_rows(cmap, ids[0], came, out)


def diag_rows(ids, cmap, came):
    return pl.pallas_call(
        diag_kernel,
        out_shape=jax.ShapeDtypeStruct((B, W), F32),
        in_specs=[SMEM, SMEM, VMEM],
        out_specs=VMEM,
        compiler_params=params(24),
        name="diag_rows",
    )(ids, cmap, came)


def spread_lane(x, k):
    return jnp.broadcast_to(x[:, k : k + 1], (8, B))


def spread_sub(x, k):
    return jnp.broadcast_to(x[k : k + 1, :], (8, B))


def eliminate_block(strips):
    sub = lax.broadcasted_iota(jnp.int32, (8, B), 0)
    lane = lax.broadcasted_iota(jnp.int32, (8, B), 1)
    strips = list(strips)
    for m in range(16):
        first = 8 * m
        inside = (lane >= first) & (lane < first + 8)
        w = strips[m]
        cols = [spread_lane(w, first + k) for k in range(8)]
        scales, rows, mults = [], [], []
        for k in range(8):
            rs = lax.rsqrt(spread_sub(cols[k], k))
            row = jnp.where(lane == first + k, rs, spread_sub(w, k) * rs)
            p = cols[k] * rs
            mult = [spread_sub(p, q) for q in range(k + 1, 8)]
            for n, q in enumerate(range(k + 1, 8)):
                cols[q] = cols[q] - p * mult[n]
            rest = jnp.where(lane == first + k, 0.0, w) - p * row
            w = jnp.where(sub > k, rest, jnp.where(sub == k, row, w))
            scales.append(rs)
            rows.append(jnp.where(inside & (lane > first + k), 0.0, row))
            mults.append(mult)
        strips[m] = w
        for s in range(m + 1, 16):
            v = strips[s]
            below = [spread_lane(v, first + k) for k in range(8)]
            v = jnp.where(inside, 0.0, v)
            for k in range(8):
                p = below[k] * scales[k]
                v = v - p * rows[k]
                for n, q in enumerate(range(k + 1, 8)):
                    below[q] = below[q] - p * mults[k][n]
            strips[s] = v
    return strips


def dot32(a, b, ca, cb):
    return lax.dot_general(
        a, b, (((ca,), (cb,)), ((), ())), precision=lax.Precision.HIGHEST, preferred_element_type=F32
    )


def piece_rows(r):
    rows = []
    for d in range(ROWS // 2):
        x = (r // 2 + ROWS // 2 - d) % (ROWS // 2)
        rows += [2 * x + r % 2, 2 * x + 1 - r % 2]
    return rows


def factor_kernel(ids, *refs):
    pieces, (w_ref, d_ref, q_ref) = refs[:ROWS], refs[ROWS:]
    row = lax.broadcasted_iota(jnp.int32, (B, B), 0)
    col = lax.broadcasted_iota(jnp.int32, (B, B), 1)
    for k, piece in zip(piece_rows(ids[0]), pieces):
        w_ref[block(k), :] = piece[...]

    def step(kb, _):
        here = block(kb)
        d_ref[...] = w_ref[here, here]
        strips = eliminate_block([d_ref[8 * s : 8 * s + 8, :] for s in range(16)])
        for s in range(16):
            d_ref[8 * s : 8 * s + 8, :] = strips[s]
        inverse = jnp.where(row >= col, d_ref[...], 0.0)
        q_ref[...] = dot32(inverse, w_ref[here, :], 1, 0)
        q_ref[:, here] = inverse

        def below(i, _):
            rows = block(i)
            w_ref[rows, here] = jnp.zeros((B, B), F32)
            w_ref[rows, :] = w_ref[rows, :] - dot32(q_ref[:, rows], q_ref[...], 0, 0)
            return 0

        lax.fori_loop(kb + 1, NB, below, 0)
        w_ref[here, :] = q_ref[...]
        w_ref[here, here] = d_ref[...]
        return 0

    lax.fori_loop(0, NB, step, 0)


def factor(ids, pieces):
    return pl.pallas_call(
        factor_kernel,
        out_shape=jax.ShapeDtypeStruct((W, W), F32),
        in_specs=[SMEM] + [VMEM] * ROWS,
        out_specs=VMEM,
        scratch_shapes=[pltpu.VMEM((B, B), F32), pltpu.VMEM((B, W), F32)],
        compiler_params=params(32),
        name="factor",
    )(ids, *pieces)


def halves(x):
    high = x.astype(BF16)
    return high, (x - high.astype(F32)).astype(BF16)


def dot_nt(a, b):
    return lax.dot_general(a, b, (((1,), (1,)), ((), ())), preferred_element_type=F32)


def dot3(ah, al, bh, bl):
    return dot_nt(ah, bh) + (dot_nt(ah, bl) + dot_nt(al, bh))


SOLVE = 256
CHUNK = 256


def solve_rows(raw, out, eh, el):
    xh, xl = halves(raw)
    for j in range(W // SOLVE):
        upto = (j + 1) * SOLVE
        rows = slice(j * SOLVE, upto)
        out[:, rows] = dot3(xh[:, :upto], xl[:, :upto], eh[rows, :upto], el[rows, :upto])


def columns_kernel(ids, w_ref, *refs):
    pieces, (eh, el, ch, cl, x) = refs[:ROWS], refs[ROWS:]
    row = lax.broadcasted_iota(jnp.int32, (B, W), 0)
    col = lax.broadcasted_iota(jnp.int32, (B, W), 1)

    def split(i, _):
        rows = block(i)
        high, low = halves(jnp.where(row + i * B >= col, w_ref[rows, :], 0.0))
        eh[rows, :] = high
        el[rows, :] = low
        return 0

    lax.fori_loop(0, NB, split, 0)
    at_row = piece_rows(ids[0])
    for n in range(0, ROWS, 2):
        pair = jnp.concatenate([pieces[n][...], pieces[n + 1][...]], axis=0)
        solve_rows(pair, x, eh, el)
        for m in range(2):
            high, low = halves(x[m * B : (m + 1) * B, :])
            ch[block(at_row[n + m]), :] = high
            cl[block(at_row[n + m]), :] = low


def columns(ids, w, pieces):
    return pl.pallas_call(
        columns_kernel,
        out_shape=(jax.ShapeDtypeStruct((W, W), BF16),) * 4,
        in_specs=[SMEM, VMEM] + [VMEM] * ROWS,
        out_specs=(VMEM,) * 4,
        scratch_shapes=[pltpu.VMEM((CHUNK, W), F32)],
        compiler_params=params(32),
        name="columns",
    )(ids, w, *pieces)


def update_kernel(ids, pattern, places, w_ref, eh, el, ch, cl, xr_ref, own_ref, *refs):
    came, (out_ref, x, held, sems) = refs[:PARTS], refs[PARTS:]
    step = pl.program_id(0)
    r, c = ids[0], ids[1]

    def visit(group, act):
        def one(quarter, _):
            child = group // 4
            slot = (child // 4 * 4 + group % 4) * COLS + child % 4 * 4 + quarter
            col = places[1, child * 4 + quarter]

            @pl.when(col >= 0)
            def _():
                copies = [
                    pltpu.make_async_copy(
                        came[part].at[slot],
                        held.at[slot, pl.ds(part * PART, PART)],
                        sems.at[slot, part],
                    )
                    for part in range(PARTS)
                ]
                act(copies, slot, col)

            return 0

        lax.fori_loop(0, 4, one, 0)

    def begin(group, _):
        def act(copies, slot, col):
            for m in copies:
                m.start()

        @pl.when(places[0, group] >= 0)
        def _():
            visit(group, act)

        return 0

    def finish(group, _):
        row = places[0, group]

        def act(copies, slot, col):
            for m in copies:
                m.wait()
            here = block(row % (CHUNK // B)), block(col)
            out_ref[here] = out_ref[here] + held[slot]

        @pl.when((row >= 0) & (row // (CHUNK // B) == step))
        def _():
            visit(group, act)

        return 0

    @pl.when(step == 0)
    def _():
        lax.fori_loop(0, 32, begin, 0)

    solve_rows(xr_ref[...], x, eh, el)
    top = (r == 0) & (step < W // CHUNK)

    @pl.when((c > 0) & top)
    def _():
        out_ref[...] = jnp.zeros_like(out_ref)

    @pl.when((c > 0) & jnp.logical_not(top))
    def _():
        high, low = halves(x[...])
        for j in range(W // SOLVE):
            cols = slice(j * SOLVE, (j + 1) * SOLVE)
            change = dot3(high, low, ch[cols, :], cl[cols, :])
            for a in range(CHUNK // B):
                for b in range(SOLVE // B):
                    rs = slice(a * B, (a + 1) * B)
                    k = j * (SOLVE // B) + b
                    cs = slice(k * B, (k + 1) * B)
                    keep = pattern[step * (CHUNK // B) + a, k].astype(F32)
                    out_ref[rs, cs] = own_ref[rs, cs] * keep - change[rs, b * B : (b + 1) * B]

    @pl.when((c == 0) & jnp.logical_not(top))
    def _():
        out_ref[...] = x[...]

    @pl.when((c == 0) & top)
    def _():
        row = lax.broadcasted_iota(jnp.int32, (CHUNK, B), 0)
        col = lax.broadcasted_iota(jnp.int32, (CHUNK, B), 1)
        for j in range(NB):
            cols = slice(j * B, (j + 1) * B)
            rows = pl.ds(pl.multiple_of(step * CHUNK, CHUNK), CHUNK)
            above = w_ref[cols, rows].T
            here = w_ref[rows, cols]
            gap = row + step * CHUNK - (col + j * B)
            out_ref[:, cols] = jnp.where(gap > 0, above, jnp.where(gap == 0, 1.0 / here, 0.0))


    lax.fori_loop(0, 32, finish, 0)


def update(ids, pattern, places, w, solved, xr, own, came):
    rows = own.shape[0]
    whole = pl.BlockSpec((W, W), lambda i: (0, 0), pipeline_mode=pl.Buffered(1))
    part = pl.BlockSpec((CHUNK, W), lambda i: (i, 0))
    return pl.pallas_call(
        update_kernel,
        grid=(rows // CHUNK,),
        out_shape=jax.ShapeDtypeStruct(own.shape, F32),
        in_specs=[SMEM, SMEM, SMEM] + [whole] * 5 + [part, part] + [HBM] * PARTS,
        out_specs=part,
        scratch_shapes=[
            pltpu.VMEM((CHUNK, W), F32),
            pltpu.VMEM((ROWS * COLS, B, B), F32),
            pltpu.SemaphoreType.DMA((ROWS * COLS, PARTS)),
        ],
        compiler_params=params(60),
        name="update",
    )(ids, pattern, places, w, *solved, xr, own, *came)


def at(r, c):
    return r * COLS + c


def after(value, first):
    return lax.optimization_barrier((value, first))[0]


def along_x(piece):
    half = ROWS // 2
    pieces = [piece]
    for d in range(1, half):
        to = [(2 * x + k, 2 * ((x + d) % half) + k) for x in range(half) for k in range(2)]
        pieces.append(lax.ppermute(piece, "prow", to))
    return pieces


def across(pieces):
    both = []
    for piece in pieces:
        both += [piece, lax.ppermute(piece, "prow", [(k, k ^ 1) for k in range(ROWS)])]
    return both


def body(child, own, pattern, cmap):
    row, col = lax.axis_index("prow"), lax.axis_index("pcol")
    moves, sends, gets = scatter_plan()
    mine = lax.dynamic_index_in_dim(jnp.asarray(gets), at(row, col), 0, keepdims=False)
    ids = jnp.stack([row, col, mine[1]]).astype(jnp.int32)
    sends = lax.dynamic_index_in_dim(jnp.asarray(sends), at(row, col), 0, keepdims=False)

    places = cmap.reshape(32, 8)
    low, high = places % 16, places % 8
    rok = (places // 16 == row) & ((row > 0) | (low >= 8))
    cok = (places // 8 == col) & (col > 0)
    places = jnp.stack(
        [jnp.max(jnp.where(rok, low, -1), axis=1), jnp.max(jnp.where(cok, high, -1), axis=1)]
    )

    *pieces, start = pack_parent(sends, pattern, own)
    small = pack_small(after(ids, start), cmap, child)
    small = lax.all_to_all(small, "prow", 0, 0, tiled=True)
    pieces = [lax.ppermute(p, AXES, m) for p, m in zip(pieces, moves)]
    bulk = list(pack(ids, cmap, child))
    first = after(bulk[0], (small, pieces[:3]))
    bulk[0] = lax.all_to_all(first, AXES, 0, 0, tiled=True)
    top = start
    for step, piece in enumerate(pieces):
        start = jnp.where(mine[0] == step, piece, start)
        top = start if step == NB - 2 else top
    parent = lax.all_to_all(after(top, bulk[0]), "prow", 0, 0, tiled=True)

    owners, diag = relay(ids, cmap, small, parent)
    diag = lax.all_gather(diag, "pcol", axis=0)
    diag = diag_rows(ids, cmap, diag)
    pivot = across(along_x(diag))
    owners = lax.all_to_all(after(owners, diag), "pcol", 0, 0, tiled=True)
    owned = owner_rows(ids, cmap, start, after(owners, pivot[2::2]))
    xr = lax.all_gather(owned, "pcol", axis=0, tiled=True)
    to = [(at(r, c), at(c % 8, 2 * r + c // 8)) for r in range(ROWS) for c in range(COLS)]
    xc = lax.ppermute(owned, AXES, to)
    bulk[1] = lax.all_to_all(after(bulk[1], (xc, pivot)), AXES, 0, 0, tiled=True)
    xc = along_x(xc)
    w = factor(ids, pivot)
    solved = columns(ids, w, across(after(xc, w)))
    return update(ids, pattern, places, w, solved, xr, own, bulk)


def solution(mesh):
    return jax.shard_map(
        body,
        mesh=mesh,
        in_specs=(P("prow", "pcol"), P("prow", "pcol"), P("prow", "pcol"), P()),
        out_specs=P("prow", "pcol"),
        check_vma=False,
    )
```

```python
import jax
import jax.numpy as jnp
import numpy as np
from jax import lax
from jax.experimental import pallas as pl
from jax.experimental.pallas import tpu as pltpu
from jax.sharding import PartitionSpec as P

B = 128
NB = 8
W = B * NB
ROWS = 8
COLS = 16
AXES = ("prow", "pcol")
F32 = jnp.float32
BF16 = jnp.bfloat16
HBM = pl.BlockSpec(memory_space=pltpu.HBM)
SMEM = pl.BlockSpec(memory_space=pltpu.SMEM)
VMEM = pl.BlockSpec(memory_space=pltpu.VMEM)
MIB = 1024 * 1024


def params(mib):
    return pltpu.CompilerParams(vmem_limit_bytes=mib * MIB)


def block(at):
    return pl.ds(pl.multiple_of(at * B, B), B)


def find(cmap, child, group, test):
    at = jnp.int32(-1)
    entry = jnp.int32(0)
    for k in range(8):
        value = cmap[child, group * 8 + k]
        hit = test(value)
        at = jnp.where(hit, k, at)
        entry = jnp.where(hit, value, entry)
    return at, entry


def scatter_plan():
    queues = {}
    for r in range(ROWS):
        for c in range(1, COLS):
            if r == 0:
                move = ((0, c // 8), 0, c % 8)
            elif c % 8 < 5:
                move = ((0, 2 * r + c // 8), 0, c % 8)
            else:
                move = ((r, 0), 1, c)
            queues.setdefault(move[0], []).append((move[1], move[2], (r, c)))
    steps = max(len(q) for q in queues.values())
    moves = [[] for _ in range(steps)]
    sends = np.zeros((ROWS * COLS, steps, 2), np.int32)
    gets = np.zeros((ROWS * COLS, 2), np.int32)
    gets[:, 0] = -1
    gets[:, 1] = 1
    for (r, c), queue in queues.items():
        turn = (r + c // 2) % len(queue) if (r, c) != (0, 0) else 0
        for step, (form, index, to) in enumerate(queue[turn:] + queue[:turn]):
            moves[step].append((at(r, c), at(*to)))
            sends[at(r, c), step] = form, index
            gets[at(*to)] = step, form
    return moves, sends, gets


def pack_parent_kernel(sends, pattern, own, *outs):
    for step, out in enumerate(outs):
        last = step == len(outs) - 1
        form = 1 if last else sends[step, 0]
        index = 0 if last else sends[step, 1]
        for j in range(NB):
            i, k = (index, j) if last else (
                jnp.where(form == 0, j, index), jnp.where(form == 0, index, j)
            )
            keep = pattern[i, k].astype(F32)
            out[j] = own[block(i), block(k)] * keep


def pack_parent(sends, pattern, own):
    return pl.pallas_call(
        pack_parent_kernel,
        out_shape=(jax.ShapeDtypeStruct((NB, B, B), F32),) * (sends.shape[0] + 1),
        in_specs=[SMEM, SMEM, VMEM],
        out_specs=(VMEM,) * (sends.shape[0] + 1),
        compiler_params=params(60),
        name="pack_parent",
    )(sends, pattern, own)


def pack_small_kernel(ids, cmap, child, small, sems):
    r, c = ids[0], ids[1]
    mine = r // 4 * 4 + c // 4
    ja, _ = find(cmap, mine, c % 4, lambda v: v < 8)
    ia, iv = find(cmap, mine, r % 4, lambda v: v < 8)
    ja = jnp.maximum(ja, 0)
    made = []
    for a in range(8):
        dst = small.at[cmap[mine, r % 4 * 8 + a] // 16, 0]
        made.append(pltpu.make_async_copy(child.at[block(a), block(ja)], dst, sems.at[a]))
    src = child.at[block(jnp.maximum(ia, 0)), block(ja)]
    made.append(pltpu.make_async_copy(src, small.at[jnp.minimum(iv, 7), 1], sems.at[8]))
    for m in made:
        m.start()
    for m in made:
        m.wait()


def pack_small(ids, cmap, child):
    return pl.pallas_call(
        pack_small_kernel,
        out_shape=jax.ShapeDtypeStruct((ROWS, 2, B, B), F32),
        in_specs=[SMEM, SMEM, VMEM],
        out_specs=HBM,
        scratch_shapes=[pltpu.SemaphoreType.DMA((9,))],
        compiler_params=params(12),
        name="pack_small",
    )(ids, cmap, child)


def pack_kernel(ids, cmap, child, bulk, sems):
    r, c = ids[0], ids[1]
    mine = r // 4 * 4 + c // 4

    def copy(n):
        a, b = n // 8, n % 8
        slot = cmap[mine, r % 4 * 8 + a] // 16 * COLS + cmap[mine, c % 4 * 8 + b] // 8
        return pltpu.make_async_copy(child.at[block(a), block(b)], bulk.at[slot], sems.at[n])

    lax.fori_loop(0, 64, lambda n, _: (copy(n).start(), 0)[1], 0)
    lax.fori_loop(0, 64, lambda n, _: (copy(n).wait(), 0)[1], 0)


def pack(ids, cmap, child):
    return pl.pallas_call(
        pack_kernel,
        out_shape=jax.ShapeDtypeStruct((ROWS * COLS, B, B), F32),
        in_specs=[SMEM, SMEM, VMEM],
        out_specs=HBM,
        scratch_shapes=[pltpu.SemaphoreType.DMA((64,))],
        compiler_params=params(60),
        name="pack",
    )(ids, cmap, child)


def relay_kernel(ids, cmap, came, parent, owners, diag, sems):
    r, c = ids[0], ids[1]
    copies = [(parent.at[0], diag.at[2])]
    for half in range(2):
        child = half * 4 + c // 4
        pick = jnp.int32(half * 4)
        for k in range(4):
            src = half * 4 + k
            _, entry = find(cmap, child, k, lambda v: v // 16 == r)
            copies.append((came.at[src, 0], owners.at[entry % 16, half]))
            at, _ = find(cmap, child, k, lambda v: v == r)
            pick = jnp.where(at >= 0, src, pick)
        copies.append((came.at[pick, 1], diag.at[half]))
    made = [pltpu.make_async_copy(s, d, sems.at[n]) for n, (s, d) in enumerate(copies)]
    for m in made:
        m.start()
    for m in made:
        m.wait()


def relay(ids, cmap, came, parent):
    return pl.pallas_call(
        relay_kernel,
        out_shape=(
            jax.ShapeDtypeStruct((COLS, 2, B, B), F32),
            jax.ShapeDtypeStruct((3, B, B), F32),
        ),
        in_specs=[SMEM, SMEM, VMEM, VMEM],
        out_specs=(HBM, HBM),
        scratch_shapes=[pltpu.SemaphoreType.DMA((11,))],
        compiler_params=params(60),
        name="relay",
    )(ids, cmap, came, parent)


def gather_rows(cmap, wanted, came, out):
    for child in range(8):
        half, quarter = child // 4, child % 4
        hit = lax.fori_loop(
            0, 32, lambda n, h: h | (cmap[child, n] == wanted).astype(jnp.int32), jnp.int32(0)
        )

        @pl.when(hit > 0)
        def _():
            for g in range(4):
                at, entry = find(cmap, child, g, lambda v: v < 8)

                @pl.when(at >= 0)
                def _():
                    where = block(jnp.minimum(entry, 7))
                    out[:, where] = out[:, where] + came[quarter * 4 + g, half]


def owner_kernel(ids, cmap, start, came, out):
    @pl.when(ids[2] == 0)
    def _():
        for k in range(NB):
            out[:, k * B : (k + 1) * B] = start[k].T

    @pl.when(ids[2] != 0)
    def _():
        for k in range(NB):
            out[:, k * B : (k + 1) * B] = start[k]

    gather_rows(cmap, ids[0] * COLS + ids[1], came, out)


def owner_rows(ids, cmap, start, came):
    return pl.pallas_call(
        owner_kernel,
        out_shape=jax.ShapeDtypeStruct((B, W), F32),
        in_specs=[SMEM, SMEM, VMEM, VMEM],
        out_specs=VMEM,
        compiler_params=params(24),
        name="owner_rows",
    )(ids, cmap, start, came)


def diag_kernel(ids, cmap, came, out):
    out[:, :B] = came[0, 2].T
    for k in range(1, NB):
        out[:, k * B : (k + 1) * B] = came[k, 2]
    gather_rows(cmap, ids[0], came, out)


def diag_rows(ids, cmap, came):
    return pl.pallas_call(
        diag_kernel,
        out_shape=jax.ShapeDtypeStruct((B, W), F32),
        in_specs=[SMEM, SMEM, VMEM],
        out_specs=VMEM,
        compiler_params=params(24),
        name="diag_rows",
    )(ids, cmap, came)


def spread_lane(x, k):
    return jnp.broadcast_to(x[:, k : k + 1], (8, B))


def spread_sub(x, k):
    return jnp.broadcast_to(x[k : k + 1, :], (8, B))


def eliminate_block(strips):
    sub = lax.broadcasted_iota(jnp.int32, (8, B), 0)
    lane = lax.broadcasted_iota(jnp.int32, (8, B), 1)
    strips = list(strips)
    for m in range(16):
        first = 8 * m
        inside = (lane >= first) & (lane < first + 8)
        w = strips[m]
        cols = [spread_lane(w, first + k) for k in range(8)]
        scales, rows, mults = [], [], []
        for k in range(8):
            rs = lax.rsqrt(spread_sub(cols[k], k))
            row = jnp.where(lane == first + k, rs, spread_sub(w, k) * rs)
            p = cols[k] * rs
            mult = [spread_sub(p, q) for q in range(k + 1, 8)]
            for n, q in enumerate(range(k + 1, 8)):
                cols[q] = cols[q] - p * mult[n]
            rest = jnp.where(lane == first + k, 0.0, w) - p * row
            w = jnp.where(sub > k, rest, jnp.where(sub == k, row, w))
            scales.append(rs)
            rows.append(jnp.where(inside & (lane > first + k), 0.0, row))
            mults.append(mult)
        strips[m] = w
        for s in range(m + 1, 16):
            v = strips[s]
            below = [spread_lane(v, first + k) for k in range(8)]
            v = jnp.where(inside, 0.0, v)
            for k in range(8):
                p = below[k] * scales[k]
                v = v - p * rows[k]
                for n, q in enumerate(range(k + 1, 8)):
                    below[q] = below[q] - p * mults[k][n]
            strips[s] = v
    return strips


def dot32(a, b, ca, cb):
    return lax.dot_general(
        a, b, (((ca,), (cb,)), ((), ())), precision=lax.Precision.HIGHEST, preferred_element_type=F32
    )


def piece_rows(r):
    rows = []
    for d in range(ROWS // 2):
        x = (r // 2 + ROWS // 2 - d) % (ROWS // 2)
        rows += [2 * x + r % 2, 2 * x + 1 - r % 2]
    return rows


def factor_kernel(ids, *refs):
    pieces, (w_ref, d_ref, q_ref) = refs[:ROWS], refs[ROWS:]
    row = lax.broadcasted_iota(jnp.int32, (B, B), 0)
    col = lax.broadcasted_iota(jnp.int32, (B, B), 1)
    for k, piece in zip(piece_rows(ids[0]), pieces):
        w_ref[block(k), :] = piece[...]

    def step(kb, _):
        here = block(kb)
        d_ref[...] = w_ref[here, here]
        strips = eliminate_block([d_ref[8 * s : 8 * s + 8, :] for s in range(16)])
        for s in range(16):
            d_ref[8 * s : 8 * s + 8, :] = strips[s]
        inverse = jnp.where(row >= col, d_ref[...], 0.0)
        q_ref[...] = dot32(inverse, w_ref[here, :], 1, 0)
        q_ref[:, here] = inverse

        def below(i, _):
            rows = block(i)
            w_ref[rows, here] = jnp.zeros((B, B), F32)
            w_ref[rows, :] = w_ref[rows, :] - dot32(q_ref[:, rows], q_ref[...], 0, 0)
            return 0

        lax.fori_loop(kb + 1, NB, below, 0)
        w_ref[here, :] = q_ref[...]
        w_ref[here, here] = d_ref[...]
        return 0

    lax.fori_loop(0, NB, step, 0)


def factor(ids, pieces):
    return pl.pallas_call(
        factor_kernel,
        out_shape=jax.ShapeDtypeStruct((W, W), F32),
        in_specs=[SMEM] + [VMEM] * ROWS,
        out_specs=VMEM,
        scratch_shapes=[pltpu.VMEM((B, B), F32), pltpu.VMEM((B, W), F32)],
        compiler_params=params(32),
        name="factor",
    )(ids, *pieces)


def halves(x):
    high = x.astype(BF16)
    return high, (x - high.astype(F32)).astype(BF16)


def dot_nt(a, b):
    return lax.dot_general(a, b, (((1,), (1,)), ((), ())), preferred_element_type=F32)


def dot3(ah, al, bh, bl):
    return dot_nt(ah, bh) + (dot_nt(ah, bl) + dot_nt(al, bh))


SOLVE = 256
CHUNK = 256


def solve_rows(raw, out, eh, el):
    xh, xl = halves(raw)
    for j in range(W // SOLVE):
        upto = (j + 1) * SOLVE
        rows = slice(j * SOLVE, upto)
        out[:, rows] = dot3(xh[:, :upto], xl[:, :upto], eh[rows, :upto], el[rows, :upto])


def columns_kernel(ids, w_ref, *refs):
    pieces, (eh, el, ch, cl, x) = refs[:ROWS], refs[ROWS:]
    row = lax.broadcasted_iota(jnp.int32, (B, W), 0)
    col = lax.broadcasted_iota(jnp.int32, (B, W), 1)

    def split(i, _):
        rows = block(i)
        high, low = halves(jnp.where(row + i * B >= col, w_ref[rows, :], 0.0))
        eh[rows, :] = high
        el[rows, :] = low
        return 0

    lax.fori_loop(0, NB, split, 0)
    at_row = piece_rows(ids[0])
    for n in range(0, ROWS, 2):
        pair = jnp.concatenate([pieces[n][...], pieces[n + 1][...]], axis=0)
        solve_rows(pair, x, eh, el)
        for m in range(2):
            high, low = halves(x[m * B : (m + 1) * B, :])
            ch[block(at_row[n + m]), :] = high
            cl[block(at_row[n + m]), :] = low


def columns(ids, w, pieces):
    return pl.pallas_call(
        columns_kernel,
        out_shape=(jax.ShapeDtypeStruct((W, W), BF16),) * 4,
        in_specs=[SMEM, VMEM] + [VMEM] * ROWS,
        out_specs=(VMEM,) * 4,
        scratch_shapes=[pltpu.VMEM((CHUNK, W), F32)],
        compiler_params=params(32),
        name="columns",
    )(ids, w, *pieces)


def update_kernel(ids, pattern, w_ref, eh, el, ch, cl, xr_ref, own_ref, out_ref, x):
    step = pl.program_id(0)
    r, c = ids[0], ids[1]
    solve_rows(xr_ref[...], x, eh, el)
    top = (r == 0) & (step < W // CHUNK)

    @pl.when((c > 0) & top)
    def _():
        out_ref[...] = jnp.zeros_like(out_ref)

    @pl.when((c > 0) & jnp.logical_not(top))
    def _():
        high, low = halves(x[...])
        for j in range(W // SOLVE):
            cols = slice(j * SOLVE, (j + 1) * SOLVE)
            change = dot3(high, low, ch[cols, :], cl[cols, :])
            for a in range(CHUNK // B):
                for b in range(SOLVE // B):
                    rs = slice(a * B, (a + 1) * B)
                    k = j * (SOLVE // B) + b
                    cs = slice(k * B, (k + 1) * B)
                    keep = pattern[step * (CHUNK // B) + a, k].astype(F32)
                    out_ref[rs, cs] = own_ref[rs, cs] * keep - change[rs, b * B : (b + 1) * B]

    @pl.when((c == 0) & jnp.logical_not(top))
    def _():
        out_ref[...] = x[...]

    @pl.when((c == 0) & top)
    def _():
        row = lax.broadcasted_iota(jnp.int32, (CHUNK, B), 0)
        col = lax.broadcasted_iota(jnp.int32, (CHUNK, B), 1)
        for j in range(NB):
            cols = slice(j * B, (j + 1) * B)
            rows = pl.ds(pl.multiple_of(step * CHUNK, CHUNK), CHUNK)
            above = w_ref[cols, rows].T
            here = w_ref[rows, cols]
            gap = row + step * CHUNK - (col + j * B)
            out_ref[:, cols] = jnp.where(gap > 0, above, jnp.where(gap == 0, 1.0 / here, 0.0))


def update(ids, pattern, w, solved, xr, own):
    rows = own.shape[0]
    whole = pl.BlockSpec((W, W), lambda i: (0, 0), pipeline_mode=pl.Buffered(1))
    part = pl.BlockSpec((CHUNK, W), lambda i: (i, 0))
    return pl.pallas_call(
        update_kernel,
        grid=(rows // CHUNK,),
        out_shape=jax.ShapeDtypeStruct(own.shape, F32),
        in_specs=[SMEM, SMEM] + [whole] * 5 + [part, part],
        out_specs=part,
        scratch_shapes=[pltpu.VMEM((CHUNK, W), F32)],
        compiler_params=params(60),
        name="update",
    )(ids, pattern, w, *solved, xr, own)


def add_kernel(places, base, came, out, held, sem):
    step = pl.program_id(0)
    load = pltpu.make_async_copy(came, held, sem)

    @pl.when(step == 0)
    def _():
        load.start()

    out[...] = base[...]

    @pl.when(step == 0)
    def _():
        load.wait()

    def group_blocks(group, _):
        row = places[0, group]

        @pl.when((row >= 0) & (row // (CHUNK // B) == step))
        def _():
            child = group // 4
            for quarter in range(4):
                slot = (child // 4 * 4 + group % 4) * COLS + child % 4 * 4 + quarter
                col = places[1, child * 4 + quarter]

                @pl.when(col >= 0)
                def _():
                    here = block(row % (CHUNK // B)), block(col)
                    out[here] = out[here] + held[slot]

        return 0

    lax.fori_loop(0, 32, group_blocks, 0)


def add(places, base, came):
    part = pl.BlockSpec((CHUNK, W), lambda i: (i, 0))
    return pl.pallas_call(
        add_kernel,
        grid=(base.shape[0] // CHUNK,),
        out_shape=jax.ShapeDtypeStruct(base.shape, F32),
        in_specs=[SMEM, part, HBM],
        out_specs=part,
        scratch_shapes=[pltpu.VMEM((ROWS * COLS, B, B), F32), pltpu.SemaphoreType.DMA(())],
        compiler_params=params(60),
        name="add",
    )(places, base, came)


def at(r, c):
    return r * COLS + c


def after(value, first):
    return lax.optimization_barrier((value, first))[0]


def along_x(piece):
    half = ROWS // 2
    pieces = [piece]
    for d in range(1, half):
        to = [(2 * x + k, 2 * ((x + d) % half) + k) for x in range(half) for k in range(2)]
        pieces.append(lax.ppermute(piece, "prow", to))
    return pieces


def across(pieces):
    both = []
    for piece in pieces:
        both += [piece, lax.ppermute(piece, "prow", [(k, k ^ 1) for k in range(ROWS)])]
    return both


def body(child, own, pattern, cmap):
    row, col = lax.axis_index("prow"), lax.axis_index("pcol")
    moves, sends, gets = scatter_plan()
    mine = lax.dynamic_index_in_dim(jnp.asarray(gets), at(row, col), 0, keepdims=False)
    ids = jnp.stack([row, col, mine[1]]).astype(jnp.int32)
    sends = lax.dynamic_index_in_dim(jnp.asarray(sends), at(row, col), 0, keepdims=False)

    places = cmap.reshape(32, 8)
    low, high = places % 16, places % 8
    rok = (places // 16 == row) & ((row > 0) | (low >= 8))
    cok = (places // 8 == col) & (col > 0)
    places = jnp.stack(
        [jnp.max(jnp.where(rok, low, -1), axis=1), jnp.max(jnp.where(cok, high, -1), axis=1)]
    )

    *pieces, start = pack_parent(sends, pattern, own)
    small = pack_small(ids, cmap, child)
    small = lax.all_to_all(small, "prow", 0, 0, tiled=True)
    top = start
    for step, piece in enumerate(pieces):
        piece = lax.ppermute(piece, AXES, moves[step])
        start = jnp.where(mine[0] == step, piece, start)
        top = start if step == NB - 2 else top
    parent = lax.all_to_all(top, "prow", 0, 0, tiled=True)

    owners, diag = relay(ids, cmap, small, parent)
    diag = lax.all_gather(diag, "pcol", axis=0)
    diag = diag_rows(ids, cmap, diag)
    pivot = across(along_x(diag))
    owners = lax.all_to_all(after(owners, diag), "pcol", 0, 0, tiled=True)
    owned = owner_rows(ids, cmap, start, after(owners, pivot[2::2]))
    xr = lax.all_gather(owned, "pcol", axis=0, tiled=True)
    to = [(at(r, c), at(c % 8, 2 * r + c // 8)) for r in range(ROWS) for c in range(COLS)]
    xc = lax.ppermute(owned, AXES, to)
    bulk = after(pack(ids, cmap, child), pivot)
    xc = along_x(xc)
    w = factor(ids, after(pivot, xc[0]))
    xc, _ = lax.optimization_barrier((xc, w))
    bulk = lax.all_to_all(after(bulk, (w, xc)), AXES, 0, 0, tiled=True)
    solved = columns(ids, w, across(xc))
    base = update(ids, pattern, w, solved, xr, own)
    return add(places, base, bulk)


def solution(mesh):
    return jax.shard_map(
        body,
        mesh=mesh,
        in_specs=(P("prow", "pcol"), P("prow", "pcol"), P("prow", "pcol"), P()),
        out_specs=P("prow", "pcol"),
        check_vma=False,
    )
```

```python
import jax
import jax.numpy as jnp
import numpy as np
from jax import lax
from jax.experimental import pallas as pl
from jax.experimental.pallas import tpu as pltpu
from jax.sharding import PartitionSpec as P

B = 128
NB = 8
W = B * NB
ROWS = 8
COLS = 16
AXES = ("prow", "pcol")
F32 = jnp.float32
BF16 = jnp.bfloat16
HBM = pl.BlockSpec(memory_space=pltpu.HBM)
SMEM = pl.BlockSpec(memory_space=pltpu.SMEM)
VMEM = pl.BlockSpec(memory_space=pltpu.VMEM)
MIB = 1024 * 1024


def params(mib):
    return pltpu.CompilerParams(vmem_limit_bytes=mib * MIB)


def block(at):
    return pl.ds(pl.multiple_of(at * B, B), B)


def find(cmap, child, group, test):
    at = jnp.int32(-1)
    entry = jnp.int32(0)
    for k in range(8):
        value = cmap[child, group * 8 + k]
        hit = test(value)
        at = jnp.where(hit, k, at)
        entry = jnp.where(hit, value, entry)
    return at, entry


def scatter_plan():
    queues = {}
    for r in range(ROWS):
        for c in range(1, COLS):
            if r == 0:
                move = ((0, c // 8), 0, c % 8)
            elif c % 8 < 5:
                move = ((0, 2 * r + c // 8), 0, c % 8)
            else:
                move = ((r, 0), 1, c)
            queues.setdefault(move[0], []).append((move[1], move[2], (r, c)))
    steps = max(len(q) for q in queues.values())
    moves = [[] for _ in range(steps)]
    sends = np.zeros((ROWS * COLS, steps, 2), np.int32)
    gets = np.zeros((ROWS * COLS, 2), np.int32)
    gets[:, 0] = -1
    gets[:, 1] = 1
    for (r, c), queue in queues.items():
        turn = (r + c // 2) % len(queue) if (r, c) != (0, 0) else 0
        for step, (form, index, to) in enumerate(queue[turn:] + queue[:turn]):
            moves[step].append((at(r, c), at(*to)))
            sends[at(r, c), step] = form, index
            gets[at(*to)] = step, form
    return moves, sends, gets


def pack_parent_kernel(sends, pattern, own, *outs):
    for step, out in enumerate(outs):
        last = step == len(outs) - 1
        form = 1 if last else sends[step, 0]
        index = 0 if last else sends[step, 1]
        for j in range(NB):
            i, k = (index, j) if last else (
                jnp.where(form == 0, j, index), jnp.where(form == 0, index, j)
            )
            keep = pattern[i, k].astype(F32)
            out[j] = own[block(i), block(k)] * keep


def pack_parent(sends, pattern, own):
    return pl.pallas_call(
        pack_parent_kernel,
        out_shape=(jax.ShapeDtypeStruct((NB, B, B), F32),) * (sends.shape[0] + 1),
        in_specs=[SMEM, SMEM, VMEM],
        out_specs=(VMEM,) * (sends.shape[0] + 1),
        compiler_params=params(60),
        name="pack_parent",
    )(sends, pattern, own)


def pack_small_kernel(ids, cmap, child, small, sems):
    r, c = ids[0], ids[1]
    mine = r // 4 * 4 + c // 4
    ja, _ = find(cmap, mine, c % 4, lambda v: v < 8)
    ia, iv = find(cmap, mine, r % 4, lambda v: v < 8)
    ja = jnp.maximum(ja, 0)
    made = []
    for a in range(8):
        dst = small.at[cmap[mine, r % 4 * 8 + a] // 16, 0]
        made.append(pltpu.make_async_copy(child.at[block(a), block(ja)], dst, sems.at[a]))
    src = child.at[block(jnp.maximum(ia, 0)), block(ja)]
    made.append(pltpu.make_async_copy(src, small.at[jnp.minimum(iv, 7), 1], sems.at[8]))
    for m in made:
        m.start()
    for m in made:
        m.wait()


def pack_small(ids, cmap, child):
    return pl.pallas_call(
        pack_small_kernel,
        out_shape=jax.ShapeDtypeStruct((ROWS, 2, B, B), F32),
        in_specs=[SMEM, SMEM, VMEM],
        out_specs=HBM,
        scratch_shapes=[pltpu.SemaphoreType.DMA((9,))],
        compiler_params=params(12),
        name="pack_small",
    )(ids, cmap, child)


def pack_kernel(ids, cmap, child, bulk, sems):
    r, c = ids[0], ids[1]
    mine = r // 4 * 4 + c // 4

    def copy(n):
        a, b = n // 8, n % 8
        slot = cmap[mine, r % 4 * 8 + a] // 16 * COLS + cmap[mine, c % 4 * 8 + b] // 8
        return pltpu.make_async_copy(child.at[block(a), block(b)], bulk.at[slot], sems.at[n])

    lax.fori_loop(0, 64, lambda n, _: (copy(n).start(), 0)[1], 0)
    lax.fori_loop(0, 64, lambda n, _: (copy(n).wait(), 0)[1], 0)


def pack(ids, cmap, child):
    return pl.pallas_call(
        pack_kernel,
        out_shape=jax.ShapeDtypeStruct((ROWS * COLS, B, B), F32),
        in_specs=[SMEM, SMEM, VMEM],
        out_specs=HBM,
        scratch_shapes=[pltpu.SemaphoreType.DMA((64,))],
        compiler_params=params(60),
        name="pack",
    )(ids, cmap, child)


def relay_kernel(ids, cmap, came, parent, owners, diag, sems):
    r, c = ids[0], ids[1]
    copies = [(parent.at[0], diag.at[2])]
    for half in range(2):
        child = half * 4 + c // 4
        pick = jnp.int32(half * 4)
        for k in range(4):
            src = half * 4 + k
            _, entry = find(cmap, child, k, lambda v: v // 16 == r)
            copies.append((came.at[src, 0], owners.at[entry % 16, half]))
            at, _ = find(cmap, child, k, lambda v: v == r)
            pick = jnp.where(at >= 0, src, pick)
        copies.append((came.at[pick, 1], diag.at[half]))
    made = [pltpu.make_async_copy(s, d, sems.at[n]) for n, (s, d) in enumerate(copies)]
    for m in made:
        m.start()
    for m in made:
        m.wait()


def relay(ids, cmap, came, parent):
    return pl.pallas_call(
        relay_kernel,
        out_shape=(
            jax.ShapeDtypeStruct((COLS, 2, B, B), F32),
            jax.ShapeDtypeStruct((3, B, B), F32),
        ),
        in_specs=[SMEM, SMEM, VMEM, VMEM],
        out_specs=(HBM, HBM),
        scratch_shapes=[pltpu.SemaphoreType.DMA((11,))],
        compiler_params=params(60),
        name="relay",
    )(ids, cmap, came, parent)


def gather_rows(cmap, wanted, came, out):
    for child in range(8):
        half, quarter = child // 4, child % 4
        hit = lax.fori_loop(
            0, 32, lambda n, h: h | (cmap[child, n] == wanted).astype(jnp.int32), jnp.int32(0)
        )

        @pl.when(hit > 0)
        def _():
            for g in range(4):
                at, entry = find(cmap, child, g, lambda v: v < 8)

                @pl.when(at >= 0)
                def _():
                    where = block(jnp.minimum(entry, 7))
                    out[:, where] = out[:, where] + came[quarter * 4 + g, half]


def owner_kernel(ids, cmap, start, came, out):
    @pl.when(ids[2] == 0)
    def _():
        for k in range(NB):
            out[:, k * B : (k + 1) * B] = start[k].T

    @pl.when(ids[2] != 0)
    def _():
        for k in range(NB):
            out[:, k * B : (k + 1) * B] = start[k]

    gather_rows(cmap, ids[0] * COLS + ids[1], came, out)


def owner_rows(ids, cmap, start, came):
    return pl.pallas_call(
        owner_kernel,
        out_shape=jax.ShapeDtypeStruct((B, W), F32),
        in_specs=[SMEM, SMEM, VMEM, VMEM],
        out_specs=VMEM,
        compiler_params=params(24),
        name="owner_rows",
    )(ids, cmap, start, came)


def diag_kernel(ids, cmap, came, out):
    out[:, :B] = came[0, 2].T
    for k in range(1, NB):
        out[:, k * B : (k + 1) * B] = came[k, 2]
    gather_rows(cmap, ids[0], came, out)


def diag_rows(ids, cmap, came):
    return pl.pallas_call(
        diag_kernel,
        out_shape=jax.ShapeDtypeStruct((B, W), F32),
        in_specs=[SMEM, SMEM, VMEM],
        out_specs=VMEM,
        compiler_params=params(24),
        name="diag_rows",
    )(ids, cmap, came)


def spread_lane(x, k):
    return jnp.broadcast_to(x[:, k : k + 1], (8, B))


def spread_sub(x, k):
    return jnp.broadcast_to(x[k : k + 1, :], (8, B))


def eliminate_block(strips):
    sub = lax.broadcasted_iota(jnp.int32, (8, B), 0)
    lane = lax.broadcasted_iota(jnp.int32, (8, B), 1)
    strips = list(strips)
    for m in range(16):
        first = 8 * m
        inside = (lane >= first) & (lane < first + 8)
        w = strips[m]
        cols = [spread_lane(w, first + k) for k in range(8)]
        scales, rows, mults = [], [], []
        for k in range(8):
            rs = lax.rsqrt(spread_sub(cols[k], k))
            row = jnp.where(lane == first + k, rs, spread_sub(w, k) * rs)
            p = cols[k] * rs
            mult = [spread_sub(p, q) for q in range(k + 1, 8)]
            for n, q in enumerate(range(k + 1, 8)):
                cols[q] = cols[q] - p * mult[n]
            rest = jnp.where(lane == first + k, 0.0, w) - p * row
            w = jnp.where(sub > k, rest, jnp.where(sub == k, row, w))
            scales.append(rs)
            rows.append(jnp.where(inside & (lane > first + k), 0.0, row))
            mults.append(mult)
        strips[m] = w
        for s in range(m + 1, 16):
            v = strips[s]
            below = [spread_lane(v, first + k) for k in range(8)]
            v = jnp.where(inside, 0.0, v)
            for k in range(8):
                p = below[k] * scales[k]
                v = v - p * rows[k]
                for n, q in enumerate(range(k + 1, 8)):
                    below[q] = below[q] - p * mults[k][n]
            strips[s] = v
    return strips


def dot32(a, b, ca, cb):
    return lax.dot_general(
        a, b, (((ca,), (cb,)), ((), ())), precision=lax.Precision.HIGHEST, preferred_element_type=F32
    )


def piece_rows(r):
    rows = []
    for d in range(ROWS // 2):
        x = (r // 2 + ROWS // 2 - d) % (ROWS // 2)
        rows += [2 * x + r % 2, 2 * x + 1 - r % 2]
    return rows


def factor_kernel(ids, *refs):
    pieces, (w_ref, d_ref, q_ref) = refs[:ROWS], refs[ROWS:]
    row = lax.broadcasted_iota(jnp.int32, (B, B), 0)
    col = lax.broadcasted_iota(jnp.int32, (B, B), 1)
    for k, piece in zip(piece_rows(ids[0]), pieces):
        w_ref[block(k), :] = piece[...]

    def step(kb, _):
        here = block(kb)
        d_ref[...] = w_ref[here, here]
        strips = eliminate_block([d_ref[8 * s : 8 * s + 8, :] for s in range(16)])
        for s in range(16):
            d_ref[8 * s : 8 * s + 8, :] = strips[s]
        inverse = jnp.where(row >= col, d_ref[...], 0.0)
        q_ref[...] = dot32(inverse, w_ref[here, :], 1, 0)
        q_ref[:, here] = inverse

        def below(i, _):
            rows = block(i)
            w_ref[rows, here] = jnp.zeros((B, B), F32)
            w_ref[rows, :] = w_ref[rows, :] - dot32(q_ref[:, rows], q_ref[...], 0, 0)
            return 0

        lax.fori_loop(kb + 1, NB, below, 0)
        w_ref[here, :] = q_ref[...]
        w_ref[here, here] = d_ref[...]
        return 0

    lax.fori_loop(0, NB, step, 0)


def factor(ids, pieces):
    return pl.pallas_call(
        factor_kernel,
        out_shape=jax.ShapeDtypeStruct((W, W), F32),
        in_specs=[SMEM] + [VMEM] * ROWS,
        out_specs=VMEM,
        scratch_shapes=[pltpu.VMEM((B, B), F32), pltpu.VMEM((B, W), F32)],
        compiler_params=params(32),
        name="factor",
    )(ids, *pieces)


def halves(x):
    high = x.astype(BF16)
    return high, (x - high.astype(F32)).astype(BF16)


def dot_nt(a, b):
    return lax.dot_general(a, b, (((1,), (1,)), ((), ())), preferred_element_type=F32)


def dot3(ah, al, bh, bl):
    return dot_nt(ah, bh) + (dot_nt(ah, bl) + dot_nt(al, bh))


SOLVE = 256
CHUNK = 256


def solve_rows(raw, out, eh, el):
    xh, xl = halves(raw)
    for j in range(W // SOLVE):
        upto = (j + 1) * SOLVE
        rows = slice(j * SOLVE, upto)
        out[:, rows] = dot3(xh[:, :upto], xl[:, :upto], eh[rows, :upto], el[rows, :upto])


def columns_kernel(ids, w_ref, *refs):
    pieces, (eh, el, ch, cl, x) = refs[:ROWS], refs[ROWS:]
    row = lax.broadcasted_iota(jnp.int32, (B, W), 0)
    col = lax.broadcasted_iota(jnp.int32, (B, W), 1)

    def split(i, _):
        rows = block(i)
        high, low = halves(jnp.where(row + i * B >= col, w_ref[rows, :], 0.0))
        eh[rows, :] = high
        el[rows, :] = low
        return 0

    lax.fori_loop(0, NB, split, 0)
    at_row = piece_rows(ids[0])
    for n in range(0, ROWS, 2):
        pair = jnp.concatenate([pieces[n][...], pieces[n + 1][...]], axis=0)
        solve_rows(pair, x, eh, el)
        for m in range(2):
            high, low = halves(x[m * B : (m + 1) * B, :])
            ch[block(at_row[n + m]), :] = high
            cl[block(at_row[n + m]), :] = low


def columns(ids, w, pieces):
    return pl.pallas_call(
        columns_kernel,
        out_shape=(jax.ShapeDtypeStruct((W, W), BF16),) * 4,
        in_specs=[SMEM, VMEM] + [VMEM] * ROWS,
        out_specs=(VMEM,) * 4,
        scratch_shapes=[pltpu.VMEM((CHUNK, W), F32)],
        compiler_params=params(32),
        name="columns",
    )(ids, w, *pieces)


def update_kernel(ids, pattern, w_ref, eh, el, ch, cl, xr_ref, own_ref, out_ref, x):
    step = pl.program_id(0)
    r, c = ids[0], ids[1]
    solve_rows(xr_ref[...], x, eh, el)
    top = (r == 0) & (step < W // CHUNK)

    @pl.when((c > 0) & top)
    def _():
        out_ref[...] = jnp.zeros_like(out_ref)

    @pl.when((c > 0) & jnp.logical_not(top))
    def _():
        high, low = halves(x[...])
        for j in range(W // SOLVE):
            cols = slice(j * SOLVE, (j + 1) * SOLVE)
            change = dot3(high, low, ch[cols, :], cl[cols, :])
            for a in range(CHUNK // B):
                for b in range(SOLVE // B):
                    rs = slice(a * B, (a + 1) * B)
                    k = j * (SOLVE // B) + b
                    cs = slice(k * B, (k + 1) * B)
                    keep = pattern[step * (CHUNK // B) + a, k].astype(F32)
                    out_ref[rs, cs] = own_ref[rs, cs] * keep - change[rs, b * B : (b + 1) * B]

    @pl.when((c == 0) & jnp.logical_not(top))
    def _():
        out_ref[...] = x[...]

    @pl.when((c == 0) & top)
    def _():
        row = lax.broadcasted_iota(jnp.int32, (CHUNK, B), 0)
        col = lax.broadcasted_iota(jnp.int32, (CHUNK, B), 1)
        for j in range(NB):
            cols = slice(j * B, (j + 1) * B)
            rows = pl.ds(pl.multiple_of(step * CHUNK, CHUNK), CHUNK)
            above = w_ref[cols, rows].T
            here = w_ref[rows, cols]
            gap = row + step * CHUNK - (col + j * B)
            out_ref[:, cols] = jnp.where(gap > 0, above, jnp.where(gap == 0, 1.0 / here, 0.0))


def update(ids, pattern, w, solved, xr, own):
    rows = own.shape[0]
    whole = pl.BlockSpec((W, W), lambda i: (0, 0), pipeline_mode=pl.Buffered(1))
    part = pl.BlockSpec((CHUNK, W), lambda i: (i, 0))
    return pl.pallas_call(
        update_kernel,
        grid=(rows // CHUNK,),
        out_shape=jax.ShapeDtypeStruct(own.shape, F32),
        in_specs=[SMEM, SMEM] + [whole] * 5 + [part, part],
        out_specs=part,
        scratch_shapes=[pltpu.VMEM((CHUNK, W), F32)],
        compiler_params=params(60),
        name="update",
    )(ids, pattern, w, *solved, xr, own)


def add_kernel(places, base, came, out, held, sem):
    step = pl.program_id(0)
    load = pltpu.make_async_copy(came, held, sem)

    @pl.when(step == 0)
    def _():
        load.start()

    out[...] = base[...]

    @pl.when(step == 0)
    def _():
        load.wait()

    def group_blocks(group, _):
        row = places[0, group]

        @pl.when((row >= 0) & (row // (CHUNK // B) == step))
        def _():
            child = group // 4
            for quarter in range(4):
                slot = (child // 4 * 4 + group % 4) * COLS + child % 4 * 4 + quarter
                col = places[1, child * 4 + quarter]

                @pl.when(col >= 0)
                def _():
                    here = block(row % (CHUNK // B)), block(col)
                    out[here] = out[here] + held[slot]

        return 0

    lax.fori_loop(0, 32, group_blocks, 0)


def add(places, base, came):
    part = pl.BlockSpec((CHUNK, W), lambda i: (i, 0))
    return pl.pallas_call(
        add_kernel,
        grid=(base.shape[0] // CHUNK,),
        out_shape=jax.ShapeDtypeStruct(base.shape, F32),
        in_specs=[SMEM, part, HBM],
        out_specs=part,
        scratch_shapes=[pltpu.VMEM((ROWS * COLS, B, B), F32), pltpu.SemaphoreType.DMA(())],
        compiler_params=params(60),
        name="add",
    )(places, base, came)


def at(r, c):
    return r * COLS + c


def after(value, first):
    return lax.optimization_barrier((value, first))[0]


def along_x(piece):
    half = ROWS // 2
    pieces = [piece]
    for d in range(1, half):
        to = [(2 * x + k, 2 * ((x + d) % half) + k) for x in range(half) for k in range(2)]
        pieces.append(lax.ppermute(piece, "prow", to))
    return pieces


def across(pieces):
    both = []
    for piece in pieces:
        both += [piece, lax.ppermute(piece, "prow", [(k, k ^ 1) for k in range(ROWS)])]
    return both


def body(child, own, pattern, cmap):
    row, col = lax.axis_index("prow"), lax.axis_index("pcol")
    moves, sends, gets = scatter_plan()
    mine = lax.dynamic_index_in_dim(jnp.asarray(gets), at(row, col), 0, keepdims=False)
    ids = jnp.stack([row, col, mine[1]]).astype(jnp.int32)
    sends = lax.dynamic_index_in_dim(jnp.asarray(sends), at(row, col), 0, keepdims=False)

    places = cmap.reshape(32, 8)
    low, high = places % 16, places % 8
    rok = (places // 16 == row) & ((row > 0) | (low >= 8))
    cok = (places // 8 == col) & (col > 0)
    places = jnp.stack(
        [jnp.max(jnp.where(rok, low, -1), axis=1), jnp.max(jnp.where(cok, high, -1), axis=1)]
    )

    *pieces, start = pack_parent(sends, pattern, own)
    small = pack_small(ids, cmap, child)
    small = lax.all_to_all(small, "prow", 0, 0, tiled=True)
    top = start
    for step, piece in enumerate(pieces):
        piece = lax.ppermute(piece, AXES, moves[step])
        start = jnp.where(mine[0] == step, piece, start)
        top = start if step == NB - 2 else top
    parent = lax.all_to_all(top, "prow", 0, 0, tiled=True)

    owners, diag = relay(ids, cmap, small, parent)
    bulk = pack(after(ids, diag), cmap, child)
    diag = lax.all_gather(diag, "pcol", axis=0)
    diag = diag_rows(ids, cmap, after(diag, bulk))
    pivot = across(along_x(diag))
    owners = lax.all_to_all(after(owners, diag), "pcol", 0, 0, tiled=True)
    owned = owner_rows(ids, cmap, start, after(owners, pivot[2::2]))
    xr = lax.all_gather(owned, "pcol", axis=0, tiled=True)
    to = [(at(r, c), at(c % 8, 2 * r + c // 8)) for r in range(ROWS) for c in range(COLS)]
    xc = lax.ppermute(owned, AXES, to)

    w = factor(ids, pivot)
    xc = after(xc, w)
    bulk = lax.all_to_all(after(bulk, (w, xc)), AXES, 0, 0, tiled=True)
    solved = columns(ids, w, across(along_x(xc)))
    base = update(ids, pattern, w, solved, xr, own)
    return add(places, base, bulk)


def solution(mesh):
    return jax.shard_map(
        body,
        mesh=mesh,
        in_specs=(P("prow", "pcol"), P("prow", "pcol"), P("prow", "pcol"), P()),
        out_specs=P("prow", "pcol"),
        check_vma=False,
    )
```

```python
import jax
import jax.numpy as jnp
import numpy as np
from jax import lax
from jax.experimental import pallas as pl
from jax.experimental.pallas import tpu as pltpu
from jax.sharding import PartitionSpec as P

B = 128
NB = 8
W = B * NB
ROWS = 8
COLS = 16
AXES = ("prow", "pcol")
F32 = jnp.float32
BF16 = jnp.bfloat16
HBM = pl.BlockSpec(memory_space=pltpu.HBM)
SMEM = pl.BlockSpec(memory_space=pltpu.SMEM)
VMEM = pl.BlockSpec(memory_space=pltpu.VMEM)
MIB = 1024 * 1024


def params(mib):
    return pltpu.CompilerParams(vmem_limit_bytes=mib * MIB)


def block(at):
    return pl.ds(pl.multiple_of(at * B, B), B)


def find(cmap, child, group, test):
    at = jnp.int32(-1)
    entry = jnp.int32(0)
    for k in range(8):
        value = cmap[child, group * 8 + k]
        hit = test(value)
        at = jnp.where(hit, k, at)
        entry = jnp.where(hit, value, entry)
    return at, entry


def scatter_plan():
    queues = {}
    for r in range(ROWS):
        for c in range(1, COLS):
            if r == 0:
                move = ((0, c // 8), 0, c % 8)
            elif c % 8 < 5:
                move = ((0, 2 * r + c // 8), 0, c % 8)
            else:
                move = ((r, 0), 1, c)
            queues.setdefault(move[0], []).append((move[1], move[2], (r, c)))
    steps = max(len(q) for q in queues.values())
    moves = [[] for _ in range(steps)]
    sends = np.zeros((ROWS * COLS, steps, 2), np.int32)
    gets = np.zeros((ROWS * COLS, 2), np.int32)
    gets[:, 0] = -1
    gets[:, 1] = 1
    for (r, c), queue in queues.items():
        turn = (r + c // 2) % len(queue) if (r, c) != (0, 0) else 0
        for step, (form, index, to) in enumerate(queue[turn:] + queue[:turn]):
            moves[step].append((at(r, c), at(*to)))
            sends[at(r, c), step] = form, index
            gets[at(*to)] = step, form
    return moves, sends, gets


def pack_parent_kernel(sends, pattern, own, *outs):
    for step, out in enumerate(outs):
        last = step == len(outs) - 1
        form = 1 if last else sends[step, 0]
        index = 0 if last else sends[step, 1]
        for j in range(NB):
            i, k = (index, j) if last else (
                jnp.where(form == 0, j, index), jnp.where(form == 0, index, j)
            )
            keep = pattern[i, k].astype(F32)
            out[j] = own[block(i), block(k)] * keep


def pack_parent(sends, pattern, own):
    return pl.pallas_call(
        pack_parent_kernel,
        out_shape=(jax.ShapeDtypeStruct((NB, B, B), F32),) * (sends.shape[0] + 1),
        in_specs=[SMEM, SMEM, VMEM],
        out_specs=(VMEM,) * (sends.shape[0] + 1),
        compiler_params=params(60),
        name="pack_parent",
    )(sends, pattern, own)


def pack_small_kernel(ids, cmap, child, small, sems):
    r, c = ids[0], ids[1]
    mine = r // 4 * 4 + c // 4
    ja, _ = find(cmap, mine, c % 4, lambda v: v < 8)
    ia, iv = find(cmap, mine, r % 4, lambda v: v < 8)
    ja = jnp.maximum(ja, 0)
    made = []
    for a in range(8):
        dst = small.at[cmap[mine, r % 4 * 8 + a] // 16, 0]
        made.append(pltpu.make_async_copy(child.at[block(a), block(ja)], dst, sems.at[a]))
    src = child.at[block(jnp.maximum(ia, 0)), block(ja)]
    made.append(pltpu.make_async_copy(src, small.at[jnp.minimum(iv, 7), 1], sems.at[8]))
    for m in made:
        m.start()
    for m in made:
        m.wait()


def pack_small(ids, cmap, child):
    return pl.pallas_call(
        pack_small_kernel,
        out_shape=jax.ShapeDtypeStruct((ROWS, 2, B, B), F32),
        in_specs=[SMEM, SMEM, VMEM],
        out_specs=HBM,
        scratch_shapes=[pltpu.SemaphoreType.DMA((9,))],
        compiler_params=params(12),
        name="pack_small",
    )(ids, cmap, child)


def pack_kernel(ids, cmap, child, bulk, sems):
    r, c = ids[0], ids[1]
    mine = r // 4 * 4 + c // 4

    def copy(n):
        a, b = n // 8, n % 8
        slot = cmap[mine, r % 4 * 8 + a] // 16 * COLS + cmap[mine, c % 4 * 8 + b] // 8
        return pltpu.make_async_copy(child.at[block(a), block(b)], bulk.at[slot], sems.at[n])

    lax.fori_loop(0, 64, lambda n, _: (copy(n).start(), 0)[1], 0)
    lax.fori_loop(0, 64, lambda n, _: (copy(n).wait(), 0)[1], 0)


def pack(ids, cmap, child):
    return pl.pallas_call(
        pack_kernel,
        out_shape=jax.ShapeDtypeStruct((ROWS * COLS, B, B), F32),
        in_specs=[SMEM, SMEM, VMEM],
        out_specs=HBM,
        scratch_shapes=[pltpu.SemaphoreType.DMA((64,))],
        compiler_params=params(60),
        name="pack",
    )(ids, cmap, child)


def relay_kernel(ids, cmap, came, parent, owners, diag, sems):
    r, c = ids[0], ids[1]
    copies = [(parent.at[0], diag.at[2])]
    for half in range(2):
        child = half * 4 + c // 4
        pick = jnp.int32(half * 4)
        for k in range(4):
            src = half * 4 + k
            _, entry = find(cmap, child, k, lambda v: v // 16 == r)
            copies.append((came.at[src, 0], owners.at[entry % 16, half]))
            at, _ = find(cmap, child, k, lambda v: v == r)
            pick = jnp.where(at >= 0, src, pick)
        copies.append((came.at[pick, 1], diag.at[half]))
    made = [pltpu.make_async_copy(s, d, sems.at[n]) for n, (s, d) in enumerate(copies)]
    for m in made:
        m.start()
    for m in made:
        m.wait()


def relay(ids, cmap, came, parent):
    return pl.pallas_call(
        relay_kernel,
        out_shape=(
            jax.ShapeDtypeStruct((COLS, 2, B, B), F32),
            jax.ShapeDtypeStruct((3, B, B), F32),
        ),
        in_specs=[SMEM, SMEM, VMEM, VMEM],
        out_specs=(HBM, HBM),
        scratch_shapes=[pltpu.SemaphoreType.DMA((11,))],
        compiler_params=params(60),
        name="relay",
    )(ids, cmap, came, parent)


def gather_rows(cmap, wanted, came, out):
    for child in range(8):
        half, quarter = child // 4, child % 4
        hit = lax.fori_loop(
            0, 32, lambda n, h: h | (cmap[child, n] == wanted).astype(jnp.int32), jnp.int32(0)
        )

        @pl.when(hit > 0)
        def _():
            for g in range(4):
                at, entry = find(cmap, child, g, lambda v: v < 8)

                @pl.when(at >= 0)
                def _():
                    where = block(jnp.minimum(entry, 7))
                    out[:, where] = out[:, where] + came[quarter * 4 + g, half]


def owner_kernel(ids, cmap, start, came, out):
    @pl.when(ids[2] == 0)
    def _():
        for k in range(NB):
            out[:, k * B : (k + 1) * B] = start[k].T

    @pl.when(ids[2] != 0)
    def _():
        for k in range(NB):
            out[:, k * B : (k + 1) * B] = start[k]

    gather_rows(cmap, ids[0] * COLS + ids[1], came, out)


def owner_rows(ids, cmap, start, came):
    return pl.pallas_call(
        owner_kernel,
        out_shape=jax.ShapeDtypeStruct((B, W), F32),
        in_specs=[SMEM, SMEM, VMEM, VMEM],
        out_specs=VMEM,
        compiler_params=params(24),
        name="owner_rows",
    )(ids, cmap, start, came)


def diag_kernel(ids, cmap, came, out):
    out[:, :B] = came[0, 2].T
    for k in range(1, NB):
        out[:, k * B : (k + 1) * B] = came[k, 2]
    gather_rows(cmap, ids[0], came, out)


def diag_rows(ids, cmap, came):
    return pl.pallas_call(
        diag_kernel,
        out_shape=jax.ShapeDtypeStruct((B, W), F32),
        in_specs=[SMEM, SMEM, VMEM],
        out_specs=VMEM,
        compiler_params=params(24),
        name="diag_rows",
    )(ids, cmap, came)


def spread_lane(x, k):
    return jnp.broadcast_to(x[:, k : k + 1], (8, B))


def spread_sub(x, k):
    return jnp.broadcast_to(x[k : k + 1, :], (8, B))


def eliminate_block(strips):
    sub = lax.broadcasted_iota(jnp.int32, (8, B), 0)
    lane = lax.broadcasted_iota(jnp.int32, (8, B), 1)
    strips = list(strips)
    for m in range(16):
        first = 8 * m
        inside = (lane >= first) & (lane < first + 8)
        w = strips[m]
        cols = [spread_lane(w, first + k) for k in range(8)]
        scales, rows, mults = [], [], []
        for k in range(8):
            rs = lax.rsqrt(spread_sub(cols[k], k))
            row = jnp.where(lane == first + k, rs, spread_sub(w, k) * rs)
            p = cols[k] * rs
            mult = [spread_sub(p, q) for q in range(k + 1, 8)]
            for n, q in enumerate(range(k + 1, 8)):
                cols[q] = cols[q] - p * mult[n]
            rest = jnp.where(lane == first + k, 0.0, w) - p * row
            w = jnp.where(sub > k, rest, jnp.where(sub == k, row, w))
            scales.append(rs)
            rows.append(jnp.where(inside & (lane > first + k), 0.0, row))
            mults.append(mult)
        strips[m] = w
        for s in range(m + 1, 16):
            v = strips[s]
            below = [spread_lane(v, first + k) for k in range(8)]
            v = jnp.where(inside, 0.0, v)
            for k in range(8):
                p = below[k] * scales[k]
                v = v - p * rows[k]
                for n, q in enumerate(range(k + 1, 8)):
                    below[q] = below[q] - p * mults[k][n]
            strips[s] = v
    return strips


def dot32(a, b, ca, cb):
    return lax.dot_general(
        a, b, (((ca,), (cb,)), ((), ())), precision=lax.Precision.HIGHEST, preferred_element_type=F32
    )


def piece_rows(r):
    rows = []
    for d in range(ROWS // 2):
        x = (r // 2 + ROWS // 2 - d) % (ROWS // 2)
        rows += [2 * x + r % 2, 2 * x + 1 - r % 2]
    return rows


def factor_kernel(ids, *refs):
    pieces, (w_ref, d_ref, q_ref) = refs[:ROWS], refs[ROWS:]
    row = lax.broadcasted_iota(jnp.int32, (B, B), 0)
    col = lax.broadcasted_iota(jnp.int32, (B, B), 1)
    for k, piece in zip(piece_rows(ids[0]), pieces):
        w_ref[block(k), :] = piece[...]

    def step(kb, _):
        here = block(kb)
        d_ref[...] = w_ref[here, here]
        strips = eliminate_block([d_ref[8 * s : 8 * s + 8, :] for s in range(16)])
        for s in range(16):
            d_ref[8 * s : 8 * s + 8, :] = strips[s]
        inverse = jnp.where(row >= col, d_ref[...], 0.0)
        q_ref[...] = dot32(inverse, w_ref[here, :], 1, 0)
        q_ref[:, here] = inverse

        def below(i, _):
            rows = block(i)
            w_ref[rows, here] = jnp.zeros((B, B), F32)
            w_ref[rows, :] = w_ref[rows, :] - dot32(q_ref[:, rows], q_ref[...], 0, 0)
            return 0

        lax.fori_loop(kb + 1, NB, below, 0)
        w_ref[here, :] = q_ref[...]
        w_ref[here, here] = d_ref[...]
        return 0

    lax.fori_loop(0, NB, step, 0)


def factor(ids, pieces):
    return pl.pallas_call(
        factor_kernel,
        out_shape=jax.ShapeDtypeStruct((W, W), F32),
        in_specs=[SMEM] + [VMEM] * ROWS,
        out_specs=VMEM,
        scratch_shapes=[pltpu.VMEM((B, B), F32), pltpu.VMEM((B, W), F32)],
        compiler_params=params(32),
        name="factor",
    )(ids, *pieces)


def halves(x):
    high = x.astype(BF16)
    return high, (x - high.astype(F32)).astype(BF16)


def dot_nt(a, b):
    return lax.dot_general(a, b, (((1,), (1,)), ((), ())), preferred_element_type=F32)


def dot3(ah, al, bh, bl):
    return dot_nt(ah, bh) + (dot_nt(ah, bl) + dot_nt(al, bh))


SOLVE = 256
CHUNK = 256


def solve_rows(raw, out, eh, el):
    xh, xl = halves(raw)
    for j in range(W // SOLVE):
        upto = (j + 1) * SOLVE
        rows = slice(j * SOLVE, upto)
        out[:, rows] = dot3(xh[:, :upto], xl[:, :upto], eh[rows, :upto], el[rows, :upto])


def columns_kernel(ids, w_ref, *refs):
    pieces, (eh, el, ch, cl, x) = refs[:ROWS], refs[ROWS:]
    row = lax.broadcasted_iota(jnp.int32, (B, W), 0)
    col = lax.broadcasted_iota(jnp.int32, (B, W), 1)

    def split(i, _):
        rows = block(i)
        high, low = halves(jnp.where(row + i * B >= col, w_ref[rows, :], 0.0))
        eh[rows, :] = high
        el[rows, :] = low
        return 0

    lax.fori_loop(0, NB, split, 0)
    at_row = piece_rows(ids[0])
    for n in range(0, ROWS, 2):
        pair = jnp.concatenate([pieces[n][...], pieces[n + 1][...]], axis=0)
        solve_rows(pair, x, eh, el)
        for m in range(2):
            high, low = halves(x[m * B : (m + 1) * B, :])
            ch[block(at_row[n + m]), :] = high
            cl[block(at_row[n + m]), :] = low


def columns(ids, w, pieces):
    return pl.pallas_call(
        columns_kernel,
        out_shape=(jax.ShapeDtypeStruct((W, W), BF16),) * 4,
        in_specs=[SMEM, VMEM] + [VMEM] * ROWS,
        out_specs=(VMEM,) * 4,
        scratch_shapes=[pltpu.VMEM((CHUNK, W), F32)],
        compiler_params=params(32),
        name="columns",
    )(ids, w, *pieces)


def update_kernel(ids, pattern, w_ref, eh, el, ch, cl, xr_ref, own_ref, out_ref, x):
    step = pl.program_id(0)
    r, c = ids[0], ids[1]
    solve_rows(xr_ref[...], x, eh, el)
    top = (r == 0) & (step < W // CHUNK)

    @pl.when((c > 0) & top)
    def _():
        out_ref[...] = jnp.zeros_like(out_ref)

    @pl.when((c > 0) & jnp.logical_not(top))
    def _():
        high, low = halves(x[...])
        for j in range(W // SOLVE):
            cols = slice(j * SOLVE, (j + 1) * SOLVE)
            change = dot3(high, low, ch[cols, :], cl[cols, :])
            for a in range(CHUNK // B):
                for b in range(SOLVE // B):
                    rs = slice(a * B, (a + 1) * B)
                    k = j * (SOLVE // B) + b
                    cs = slice(k * B, (k + 1) * B)
                    keep = pattern[step * (CHUNK // B) + a, k].astype(F32)
                    out_ref[rs, cs] = own_ref[rs, cs] * keep - change[rs, b * B : (b + 1) * B]

    @pl.when((c == 0) & jnp.logical_not(top))
    def _():
        out_ref[...] = x[...]

    @pl.when((c == 0) & top)
    def _():
        row = lax.broadcasted_iota(jnp.int32, (CHUNK, B), 0)
        col = lax.broadcasted_iota(jnp.int32, (CHUNK, B), 1)
        for j in range(NB):
            cols = slice(j * B, (j + 1) * B)
            rows = pl.ds(pl.multiple_of(step * CHUNK, CHUNK), CHUNK)
            above = w_ref[cols, rows].T
            here = w_ref[rows, cols]
            gap = row + step * CHUNK - (col + j * B)
            out_ref[:, cols] = jnp.where(gap > 0, above, jnp.where(gap == 0, 1.0 / here, 0.0))


def update(ids, pattern, w, solved, xr, own):
    rows = own.shape[0]
    whole = pl.BlockSpec((W, W), lambda i: (0, 0), pipeline_mode=pl.Buffered(1))
    part = pl.BlockSpec((CHUNK, W), lambda i: (i, 0))
    return pl.pallas_call(
        update_kernel,
        grid=(rows // CHUNK,),
        out_shape=jax.ShapeDtypeStruct(own.shape, F32),
        in_specs=[SMEM, SMEM] + [whole] * 5 + [part, part],
        out_specs=part,
        scratch_shapes=[pltpu.VMEM((CHUNK, W), F32)],
        compiler_params=params(60),
        name="update",
    )(ids, pattern, w, *solved, xr, own)


def add_kernel(places, base, came, out, held, sem):
    step = pl.program_id(0)
    load = pltpu.make_async_copy(came, held, sem)

    @pl.when(step == 0)
    def _():
        load.start()

    out[...] = base[...]

    @pl.when(step == 0)
    def _():
        load.wait()

    def group_blocks(group, _):
        row = places[0, group]

        @pl.when((row >= 0) & (row // (CHUNK // B) == step))
        def _():
            child = group // 4
            for quarter in range(4):
                slot = (child // 4 * 4 + group % 4) * COLS + child % 4 * 4 + quarter
                col = places[1, child * 4 + quarter]

                @pl.when(col >= 0)
                def _():
                    here = block(row % (CHUNK // B)), block(col)
                    out[here] = out[here] + held[slot]

        return 0

    lax.fori_loop(0, 32, group_blocks, 0)


def add(places, base, came):
    part = pl.BlockSpec((CHUNK, W), lambda i: (i, 0))
    return pl.pallas_call(
        add_kernel,
        grid=(base.shape[0] // CHUNK,),
        out_shape=jax.ShapeDtypeStruct(base.shape, F32),
        in_specs=[SMEM, part, HBM],
        out_specs=part,
        scratch_shapes=[pltpu.VMEM((ROWS * COLS, B, B), F32), pltpu.SemaphoreType.DMA(())],
        compiler_params=params(60),
        name="add",
    )(places, base, came)


def at(r, c):
    return r * COLS + c


def after(value, first):
    return lax.optimization_barrier((value, first))[0]


def along_x(piece):
    half = ROWS // 2
    pieces = [piece]
    for d in range(1, half):
        to = [(2 * x + k, 2 * ((x + d) % half) + k) for x in range(half) for k in range(2)]
        pieces.append(lax.ppermute(piece, "prow", to))
    return pieces


def across(pieces):
    both = []
    for piece in pieces:
        both += [piece, lax.ppermute(piece, "prow", [(k, k ^ 1) for k in range(ROWS)])]
    return both


def body(child, own, pattern, cmap):
    row, col = lax.axis_index("prow"), lax.axis_index("pcol")
    moves, sends, gets = scatter_plan()
    mine = lax.dynamic_index_in_dim(jnp.asarray(gets), at(row, col), 0, keepdims=False)
    ids = jnp.stack([row, col, mine[1]]).astype(jnp.int32)
    sends = lax.dynamic_index_in_dim(jnp.asarray(sends), at(row, col), 0, keepdims=False)

    places = cmap.reshape(32, 8)
    low, high = places % 16, places % 8
    rok = (places // 16 == row) & ((row > 0) | (low >= 8))
    cok = (places // 8 == col) & (col > 0)
    places = jnp.stack(
        [jnp.max(jnp.where(rok, low, -1), axis=1), jnp.max(jnp.where(cok, high, -1), axis=1)]
    )

    *pieces, start = pack_parent(sends, pattern, own)
    small = pack_small(ids, cmap, child)
    small = lax.all_to_all(small, "prow", 0, 0, tiled=True)
    top = start
    for step, piece in enumerate(pieces):
        piece = lax.ppermute(piece, AXES, moves[step])
        start = jnp.where(mine[0] == step, piece, start)
        top = start if step == NB - 2 else top
    parent = lax.all_to_all(top, "prow", 0, 0, tiled=True)

    owners, diag = relay(ids, cmap, small, parent)
    bulk = pack(after(ids, diag), cmap, child)
    diag = lax.all_gather(diag, "pcol", axis=0)
    diag = diag_rows(ids, cmap, after(diag, bulk))
    pivot = across(along_x(diag))
    owners = lax.all_to_all(after(owners, diag), "pcol", 0, 0, tiled=True)
    owned = owner_rows(ids, cmap, start, after(owners, pivot[2::2]))
    to = [(at(r, c), at(c % 8, 2 * r + c // 8)) for r in range(ROWS) for c in range(COLS)]
    xc = lax.ppermute(owned, AXES, to)
    xr = lax.all_gather(after(owned, xc), "pcol", axis=0, tiled=True)

    w = factor(ids, after(pivot, xc))
    xc, _ = lax.optimization_barrier((along_x(xc), w))
    bulk = lax.all_to_all(after(bulk, (w, xc)), AXES, 0, 0, tiled=True)
    solved = columns(ids, w, across(xc))
    base = update(ids, pattern, w, solved, xr, own)
    return add(places, base, bulk)


def solution(mesh):
    return jax.shard_map(
        body,
        mesh=mesh,
        in_specs=(P("prow", "pcol"), P("prow", "pcol"), P("prow", "pcol"), P()),
        out_specs=P("prow", "pcol"),
        check_vma=False,
    )
```

```python
import jax
import jax.numpy as jnp
import numpy as np
from jax import lax
from jax.experimental import pallas as pl
from jax.experimental.pallas import tpu as pltpu
from jax.sharding import PartitionSpec as P

B = 128
NB = 8
W = B * NB
ROWS = 8
COLS = 16
AXES = ("prow", "pcol")
F32 = jnp.float32
BF16 = jnp.bfloat16
HBM = pl.BlockSpec(memory_space=pltpu.HBM)
SMEM = pl.BlockSpec(memory_space=pltpu.SMEM)
VMEM = pl.BlockSpec(memory_space=pltpu.VMEM)
MIB = 1024 * 1024


def params(mib):
    return pltpu.CompilerParams(vmem_limit_bytes=mib * MIB)


def block(at):
    return pl.ds(pl.multiple_of(at * B, B), B)


def find(cmap, child, group, test):
    at = jnp.int32(-1)
    entry = jnp.int32(0)
    for k in range(8):
        value = cmap[child, group * 8 + k]
        hit = test(value)
        at = jnp.where(hit, k, at)
        entry = jnp.where(hit, value, entry)
    return at, entry


def scatter_plan():
    queues = {}
    for r in range(ROWS):
        for c in range(1, COLS):
            if r == 0:
                move = ((0, c // 8), 0, c % 8)
            elif c % 8 < 5:
                move = ((0, 2 * r + c // 8), 0, c % 8)
            else:
                move = ((r, 0), 1, c)
            queues.setdefault(move[0], []).append((move[1], move[2], (r, c)))
    steps = max(len(q) for q in queues.values())
    moves = [[] for _ in range(steps)]
    sends = np.zeros((ROWS * COLS, steps, 2), np.int32)
    gets = np.zeros((ROWS * COLS, 2), np.int32)
    gets[:, 0] = -1
    gets[:, 1] = 1
    for (r, c), queue in queues.items():
        turn = (r + c // 2) % len(queue) if (r, c) != (0, 0) else 0
        for step, (form, index, to) in enumerate(queue[turn:] + queue[:turn]):
            moves[step].append((at(r, c), at(*to)))
            sends[at(r, c), step] = form, index
            gets[at(*to)] = step, form
    return moves, sends, gets


def pack_parent_kernel(sends, pattern, own, *outs):
    for step, out in enumerate(outs):
        last = step == len(outs) - 1
        form = 1 if last else sends[step, 0]
        index = 0 if last else sends[step, 1]
        for j in range(NB):
            i, k = (index, j) if last else (
                jnp.where(form == 0, j, index), jnp.where(form == 0, index, j)
            )
            keep = pattern[i, k].astype(F32)
            out[j] = own[block(i), block(k)] * keep


def pack_parent(sends, pattern, own):
    return pl.pallas_call(
        pack_parent_kernel,
        out_shape=(jax.ShapeDtypeStruct((NB, B, B), F32),) * (sends.shape[0] + 1),
        in_specs=[SMEM, SMEM, VMEM],
        out_specs=(VMEM,) * (sends.shape[0] + 1),
        compiler_params=params(60),
        name="pack_parent",
    )(sends, pattern, own)


def pack_small_kernel(ids, cmap, child, small, sems):
    r, c = ids[0], ids[1]
    mine = r // 4 * 4 + c // 4
    ja, _ = find(cmap, mine, c % 4, lambda v: v < 8)
    ia, iv = find(cmap, mine, r % 4, lambda v: v < 8)
    ja = jnp.maximum(ja, 0)
    made = []
    for a in range(8):
        dst = small.at[cmap[mine, r % 4 * 8 + a] // 16, 0]
        made.append(pltpu.make_async_copy(child.at[block(a), block(ja)], dst, sems.at[a]))
    src = child.at[block(jnp.maximum(ia, 0)), block(ja)]
    made.append(pltpu.make_async_copy(src, small.at[jnp.minimum(iv, 7), 1], sems.at[8]))
    for m in made:
        m.start()
    for m in made:
        m.wait()


def pack_small(ids, cmap, child):
    return pl.pallas_call(
        pack_small_kernel,
        out_shape=jax.ShapeDtypeStruct((ROWS, 2, B, B), F32),
        in_specs=[SMEM, SMEM, VMEM],
        out_specs=HBM,
        scratch_shapes=[pltpu.SemaphoreType.DMA((9,))],
        compiler_params=params(12),
        name="pack_small",
    )(ids, cmap, child)


def pack_kernel(ids, cmap, child, bulk, sems):
    r, c = ids[0], ids[1]
    mine = r // 4 * 4 + c // 4

    def copy(n):
        a, b = n // 8, n % 8
        slot = cmap[mine, r % 4 * 8 + a] // 16 * COLS + cmap[mine, c % 4 * 8 + b] // 8
        return pltpu.make_async_copy(child.at[block(a), block(b)], bulk.at[slot], sems.at[n])

    lax.fori_loop(0, 64, lambda n, _: (copy(n).start(), 0)[1], 0)
    lax.fori_loop(0, 64, lambda n, _: (copy(n).wait(), 0)[1], 0)


def pack(ids, cmap, child):
    return pl.pallas_call(
        pack_kernel,
        out_shape=jax.ShapeDtypeStruct((ROWS * COLS, B, B), F32),
        in_specs=[SMEM, SMEM, VMEM],
        out_specs=HBM,
        scratch_shapes=[pltpu.SemaphoreType.DMA((64,))],
        compiler_params=params(60),
        name="pack",
    )(ids, cmap, child)


def relay_kernel(ids, cmap, came, parent, owners, diag, sems):
    r, c = ids[0], ids[1]
    copies = [(parent.at[0], diag.at[2])]
    for half in range(2):
        child = half * 4 + c // 4
        pick = jnp.int32(half * 4)
        for k in range(4):
            src = half * 4 + k
            _, entry = find(cmap, child, k, lambda v: v // 16 == r)
            copies.append((came.at[src, 0], owners.at[entry % 16, half]))
            at, _ = find(cmap, child, k, lambda v: v == r)
            pick = jnp.where(at >= 0, src, pick)
        copies.append((came.at[pick, 1], diag.at[half]))
    made = [pltpu.make_async_copy(s, d, sems.at[n]) for n, (s, d) in enumerate(copies)]
    for m in made:
        m.start()
    for m in made:
        m.wait()


def relay(ids, cmap, came, parent):
    return pl.pallas_call(
        relay_kernel,
        out_shape=(
            jax.ShapeDtypeStruct((COLS, 2, B, B), F32),
            jax.ShapeDtypeStruct((3, B, B), F32),
        ),
        in_specs=[SMEM, SMEM, VMEM, VMEM],
        out_specs=(HBM, HBM),
        scratch_shapes=[pltpu.SemaphoreType.DMA((11,))],
        compiler_params=params(60),
        name="relay",
    )(ids, cmap, came, parent)


def gather_rows(cmap, wanted, came, out):
    for child in range(8):
        half, quarter = child // 4, child % 4
        hit = lax.fori_loop(
            0, 32, lambda n, h: h | (cmap[child, n] == wanted).astype(jnp.int32), jnp.int32(0)
        )

        @pl.when(hit > 0)
        def _():
            for g in range(4):
                at, entry = find(cmap, child, g, lambda v: v < 8)

                @pl.when(at >= 0)
                def _():
                    where = block(jnp.minimum(entry, 7))
                    out[:, where] = out[:, where] + came[quarter * 4 + g, half]


def owner_kernel(ids, cmap, start, came, out):
    @pl.when(ids[2] == 0)
    def _():
        for k in range(NB):
            out[:, k * B : (k + 1) * B] = start[k].T

    @pl.when(ids[2] != 0)
    def _():
        for k in range(NB):
            out[:, k * B : (k + 1) * B] = start[k]

    gather_rows(cmap, ids[0] * COLS + ids[1], came, out)


def owner_rows(ids, cmap, start, came):
    return pl.pallas_call(
        owner_kernel,
        out_shape=jax.ShapeDtypeStruct((B, W), F32),
        in_specs=[SMEM, SMEM, VMEM, VMEM],
        out_specs=VMEM,
        compiler_params=params(24),
        name="owner_rows",
    )(ids, cmap, start, came)


def diag_kernel(ids, cmap, came, out):
    out[:, :B] = came[0, 2].T
    for k in range(1, NB):
        out[:, k * B : (k + 1) * B] = came[k, 2]
    gather_rows(cmap, ids[0], came, out)


def diag_rows(ids, cmap, came):
    return pl.pallas_call(
        diag_kernel,
        out_shape=jax.ShapeDtypeStruct((B, W), F32),
        in_specs=[SMEM, SMEM, VMEM],
        out_specs=VMEM,
        compiler_params=params(24),
        name="diag_rows",
    )(ids, cmap, came)


def spread_lane(x, k):
    return jnp.broadcast_to(x[:, k : k + 1], (8, B))


def spread_sub(x, k):
    return jnp.broadcast_to(x[k : k + 1, :], (8, B))


def eliminate_block(strips):
    sub = lax.broadcasted_iota(jnp.int32, (8, B), 0)
    lane = lax.broadcasted_iota(jnp.int32, (8, B), 1)
    strips = list(strips)
    for m in range(16):
        first = 8 * m
        inside = (lane >= first) & (lane < first + 8)
        w = strips[m]
        cols = [spread_lane(w, first + k) for k in range(8)]
        scales, rows, mults = [], [], []
        for k in range(8):
            rs = lax.rsqrt(spread_sub(cols[k], k))
            row = jnp.where(lane == first + k, rs, spread_sub(w, k) * rs)
            p = cols[k] * rs
            mult = [spread_sub(p, q) for q in range(k + 1, 8)]
            for n, q in enumerate(range(k + 1, 8)):
                cols[q] = cols[q] - p * mult[n]
            rest = jnp.where(lane == first + k, 0.0, w) - p * row
            w = jnp.where(sub > k, rest, jnp.where(sub == k, row, w))
            scales.append(rs)
            rows.append(jnp.where(inside & (lane > first + k), 0.0, row))
            mults.append(mult)
        strips[m] = w
        for s in range(m + 1, 16):
            v = strips[s]
            below = [spread_lane(v, first + k) for k in range(8)]
            v = jnp.where(inside, 0.0, v)
            for k in range(8):
                p = below[k] * scales[k]
                v = v - p * rows[k]
                for n, q in enumerate(range(k + 1, 8)):
                    below[q] = below[q] - p * mults[k][n]
            strips[s] = v
    return strips


def dot32(a, b, ca, cb):
    return lax.dot_general(
        a, b, (((ca,), (cb,)), ((), ())), precision=lax.Precision.HIGHEST, preferred_element_type=F32
    )


def piece_rows(r):
    rows = []
    for d in range(ROWS // 2):
        x = (r // 2 + ROWS // 2 - d) % (ROWS // 2)
        rows += [2 * x + r % 2, 2 * x + 1 - r % 2]
    return rows


def factor_kernel(ids, *refs):
    pieces, (w_ref, d_ref, q_ref) = refs[:ROWS], refs[ROWS:]
    row = lax.broadcasted_iota(jnp.int32, (B, B), 0)
    col = lax.broadcasted_iota(jnp.int32, (B, B), 1)
    for k, piece in zip(piece_rows(ids[0]), pieces):
        w_ref[block(k), :] = piece[...]

    def step(kb, _):
        here = block(kb)
        d_ref[...] = w_ref[here, here]
        strips = eliminate_block([d_ref[8 * s : 8 * s + 8, :] for s in range(16)])
        for s in range(16):
            d_ref[8 * s : 8 * s + 8, :] = strips[s]
        inverse = jnp.where(row >= col, d_ref[...], 0.0)
        q_ref[...] = dot32(inverse, w_ref[here, :], 1, 0)
        q_ref[:, here] = inverse

        def below(i, _):
            rows = block(i)
            w_ref[rows, here] = jnp.zeros((B, B), F32)
            w_ref[rows, :] = w_ref[rows, :] - dot32(q_ref[:, rows], q_ref[...], 0, 0)
            return 0

        lax.fori_loop(kb + 1, NB, below, 0)
        w_ref[here, :] = q_ref[...]
        w_ref[here, here] = d_ref[...]
        return 0

    lax.fori_loop(0, NB, step, 0)


def factor(ids, pieces):
    return pl.pallas_call(
        factor_kernel,
        out_shape=jax.ShapeDtypeStruct((W, W), F32),
        in_specs=[SMEM] + [VMEM] * ROWS,
        out_specs=VMEM,
        scratch_shapes=[pltpu.VMEM((B, B), F32), pltpu.VMEM((B, W), F32)],
        compiler_params=params(32),
        name="factor",
    )(ids, *pieces)


def halves(x):
    high = x.astype(BF16)
    return high, (x - high.astype(F32)).astype(BF16)


def dot_nt(a, b):
    return lax.dot_general(a, b, (((1,), (1,)), ((), ())), preferred_element_type=F32)


def dot3(ah, al, bh, bl):
    return dot_nt(ah, bh) + (dot_nt(ah, bl) + dot_nt(al, bh))


SOLVE = 256
CHUNK = 256


def solve_rows(raw, out, eh, el):
    xh, xl = halves(raw)
    for j in range(W // SOLVE):
        upto = (j + 1) * SOLVE
        rows = slice(j * SOLVE, upto)
        out[:, rows] = dot3(xh[:, :upto], xl[:, :upto], eh[rows, :upto], el[rows, :upto])


def columns_kernel(ids, w_ref, *refs):
    pieces, (eh, el, ch, cl, x) = refs[:ROWS], refs[ROWS:]
    row = lax.broadcasted_iota(jnp.int32, (B, W), 0)
    col = lax.broadcasted_iota(jnp.int32, (B, W), 1)

    def split(i, _):
        rows = block(i)
        high, low = halves(jnp.where(row + i * B >= col, w_ref[rows, :], 0.0))
        eh[rows, :] = high
        el[rows, :] = low
        return 0

    lax.fori_loop(0, NB, split, 0)
    at_row = piece_rows(ids[0])
    for n in range(0, ROWS, 2):
        pair = jnp.concatenate([pieces[n][...], pieces[n + 1][...]], axis=0)
        solve_rows(pair, x, eh, el)
        for m in range(2):
            high, low = halves(x[m * B : (m + 1) * B, :])
            ch[block(at_row[n + m]), :] = high
            cl[block(at_row[n + m]), :] = low


def columns(ids, w, pieces):
    return pl.pallas_call(
        columns_kernel,
        out_shape=(jax.ShapeDtypeStruct((W, W), BF16),) * 4,
        in_specs=[SMEM, VMEM] + [VMEM] * ROWS,
        out_specs=(VMEM,) * 4,
        scratch_shapes=[pltpu.VMEM((CHUNK, W), F32)],
        compiler_params=params(32),
        name="columns",
    )(ids, w, *pieces)


def update_kernel(ids, pattern, w_ref, eh, el, ch, cl, xr_ref, own_ref, out_ref, x):
    step = pl.program_id(0)
    r, c = ids[0], ids[1]
    solve_rows(xr_ref[...], x, eh, el)
    top = (r == 0) & (step < W // CHUNK)

    @pl.when((c > 0) & top)
    def _():
        out_ref[...] = jnp.zeros_like(out_ref)

    @pl.when((c > 0) & jnp.logical_not(top))
    def _():
        high, low = halves(x[...])
        for j in range(W // SOLVE):
            cols = slice(j * SOLVE, (j + 1) * SOLVE)
            change = dot3(high, low, ch[cols, :], cl[cols, :])
            for a in range(CHUNK // B):
                for b in range(SOLVE // B):
                    rs = slice(a * B, (a + 1) * B)
                    k = j * (SOLVE // B) + b
                    cs = slice(k * B, (k + 1) * B)
                    keep = pattern[step * (CHUNK // B) + a, k].astype(F32)
                    out_ref[rs, cs] = own_ref[rs, cs] * keep - change[rs, b * B : (b + 1) * B]

    @pl.when((c == 0) & jnp.logical_not(top))
    def _():
        out_ref[...] = x[...]

    @pl.when((c == 0) & top)
    def _():
        row = lax.broadcasted_iota(jnp.int32, (CHUNK, B), 0)
        col = lax.broadcasted_iota(jnp.int32, (CHUNK, B), 1)
        for j in range(NB):
            cols = slice(j * B, (j + 1) * B)
            rows = pl.ds(pl.multiple_of(step * CHUNK, CHUNK), CHUNK)
            above = w_ref[cols, rows].T
            here = w_ref[rows, cols]
            gap = row + step * CHUNK - (col + j * B)
            out_ref[:, cols] = jnp.where(gap > 0, above, jnp.where(gap == 0, 1.0 / here, 0.0))


def update(ids, pattern, w, solved, xr, own):
    rows = own.shape[0]
    whole = pl.BlockSpec((W, W), lambda i: (0, 0), pipeline_mode=pl.Buffered(1))
    part = pl.BlockSpec((CHUNK, W), lambda i: (i, 0))
    return pl.pallas_call(
        update_kernel,
        grid=(rows // CHUNK,),
        out_shape=jax.ShapeDtypeStruct(own.shape, F32),
        in_specs=[SMEM, SMEM] + [whole] * 5 + [part, part],
        out_specs=part,
        scratch_shapes=[pltpu.VMEM((CHUNK, W), F32)],
        compiler_params=params(60),
        name="update",
    )(ids, pattern, w, *solved, xr, own)


def add_kernel(places, base, came, out, held, sem):
    step = pl.program_id(0)
    load = pltpu.make_async_copy(came, held, sem)

    @pl.when(step == 0)
    def _():
        load.start()

    out[...] = base[...]

    @pl.when(step == 0)
    def _():
        load.wait()

    def group_blocks(group, _):
        row = places[0, group]

        @pl.when((row >= 0) & (row // (CHUNK // B) == step))
        def _():
            child = group // 4
            for quarter in range(4):
                slot = (child // 4 * 4 + group % 4) * COLS + child % 4 * 4 + quarter
                col = places[1, child * 4 + quarter]

                @pl.when(col >= 0)
                def _():
                    here = block(row % (CHUNK // B)), block(col)
                    out[here] = out[here] + held[slot]

        return 0

    lax.fori_loop(0, 32, group_blocks, 0)


def add(places, base, came):
    part = pl.BlockSpec((CHUNK, W), lambda i: (i, 0))
    return pl.pallas_call(
        add_kernel,
        grid=(base.shape[0] // CHUNK,),
        out_shape=jax.ShapeDtypeStruct(base.shape, F32),
        in_specs=[SMEM, part, HBM],
        out_specs=part,
        scratch_shapes=[pltpu.VMEM((ROWS * COLS, B, B), F32), pltpu.SemaphoreType.DMA(())],
        compiler_params=params(60),
        name="add",
    )(places, base, came)


def at(r, c):
    return r * COLS + c


def after(value, first):
    return lax.optimization_barrier((value, first))[0]


def along_x(piece):
    half = ROWS // 2
    pieces = [piece]
    for d in range(1, half):
        to = [(2 * x + k, 2 * ((x + d) % half) + k) for x in range(half) for k in range(2)]
        pieces.append(lax.ppermute(piece, "prow", to))
    return pieces


def across(pieces):
    both = []
    for piece in pieces:
        both += [piece, lax.ppermute(piece, "prow", [(k, k ^ 1) for k in range(ROWS)])]
    return both


def body(child, own, pattern, cmap):
    row, col = lax.axis_index("prow"), lax.axis_index("pcol")
    moves, sends, gets = scatter_plan()
    mine = lax.dynamic_index_in_dim(jnp.asarray(gets), at(row, col), 0, keepdims=False)
    ids = jnp.stack([row, col, mine[1]]).astype(jnp.int32)
    sends = lax.dynamic_index_in_dim(jnp.asarray(sends), at(row, col), 0, keepdims=False)

    places = cmap.reshape(32, 8)
    low, high = places % 16, places % 8
    rok = (places // 16 == row) & ((row > 0) | (low >= 8))
    cok = (places // 8 == col) & (col > 0)
    places = jnp.stack(
        [jnp.max(jnp.where(rok, low, -1), axis=1), jnp.max(jnp.where(cok, high, -1), axis=1)]
    )

    *pieces, start = pack_parent(sends, pattern, own)
    small = pack_small(ids, cmap, child)
    small = lax.all_to_all(small, "prow", 0, 0, tiled=True)
    top = start
    for step, piece in enumerate(pieces):
        piece = lax.ppermute(piece, AXES, moves[step])
        start = jnp.where(mine[0] == step, piece, start)
        top = start if step == NB - 2 else top
    parent = lax.all_to_all(top, "prow", 0, 0, tiled=True)

    owners, diag = relay(ids, cmap, small, parent)
    bulk = pack(after(ids, diag), cmap, child)
    diag = lax.all_gather(diag, "pcol", axis=0)
    diag = diag_rows(ids, cmap, after(diag, bulk))
    pivot = across(along_x(diag))
    owners = lax.all_to_all(after(owners, diag), "pcol", 0, 0, tiled=True)
    owned = owner_rows(ids, cmap, start, after(owners, pivot[2::2]))
    to = [(at(r, c), at(c % 8, 2 * r + c // 8)) for r in range(ROWS) for c in range(COLS)]
    xc = lax.ppermute(owned, AXES, to)
    xr = lax.all_gather(owned, "pcol", axis=0, tiled=True)

    w = factor(ids, pivot)
    xc = along_x(after(xc, w))
    bulk = lax.all_to_all(after(bulk, (w, xc)), AXES, 0, 0, tiled=True)
    solved = columns(ids, w, across(xc))
    base = update(ids, pattern, w, solved, xr, own)
    return add(places, base, bulk)


def solution(mesh):
    return jax.shard_map(
        body,
        mesh=mesh,
        in_specs=(P("prow", "pcol"), P("prow", "pcol"), P("prow", "pcol"), P()),
        out_specs=P("prow", "pcol"),
        check_vma=False,
    )
```
